32 devices in a mesh: user: 8 (over z, y), feat: 4 (over x, core).
Axes of the slice: x: 2, y: 2, z: 4, core: 2. Of those that a mesh axis runs over, the one named last changes fastest.
Arguments:
- view_one: bfloat16 [1024, 2048], P('user', 'feat'), may hold values from -8 to 8
- view_two: bfloat16 [1024, 2048], P('user', 'feat'), may hold values from -8 to 8
- partner: int32 [1024], P('user'), may hold values from 0 to 1023, each once
Outputs:
- grad_one: float32 [1024, 2048], P('user', 'feat')
- grad_two: float32 [1024, 2048], P('user', 'feat')
The draws below stay inside these ranges and needn't reach their ends.
Inputs may be any that keep to these rules, and one draw needn't show every extreme that they name: `partner`: each index of view_two appears exactly once.
All inputs are finite; a program needn't handle non-finite values.
Results may differ from the reference program's by a relative error of at most 0.0028.
Values may be sent and summed in bfloat16 or wider, within the bound.
A program may use at most 128 MiB of HBM per device.

```python
import math
import jax
import jax.numpy as jnp
from jax import lax

D = 2048
USERS = 1024


def aligned_bases(key):
    signs = jax.random.bernoulli(key, 0.5, (8, D))
    return jnp.where(signs, 1.0, -1.0).astype(jnp.float32)


def drawn_rows(offset):
    stride_rows = USERS // 8
    row_index = jnp.arange(USERS)
    chosen = row_index % stride_rows == offset
    which = jnp.minimum(row_index // stride_rows, 7)
    return (chosen, which)


def drawn_strength(which):
    target = 120.0 + 40.0 * which.astype(jnp.float32)
    return jnp.sqrt(target / (2.0 * math.sqrt(D)))


def draw_view_one(key, part):
    bases = aligned_bases(key)
    key = jax.random.fold_in(key, 3)
    values = jnp.clip(jax.random.normal(key, (USERS, D), jnp.float32), -6.0, 6.0)
    chosen, which = drawn_rows(0)
    strength = drawn_strength(which)
    values = jnp.where(chosen[:, None], strength[:, None] * bases[which], values)
    return values.astype(jnp.bfloat16)


def draw_view_two(key, part):
    bases = aligned_bases(key)
    key = jax.random.fold_in(key, 7)
    values = jnp.clip(jax.random.normal(key, (USERS, D), jnp.float32), -6.0, 6.0)
    noise = jnp.clip(jax.random.normal(jax.random.fold_in(key, 13), (USERS, D), jnp.float32), -3.0, 3.0)
    half_stride = USERS // 16
    chosen, which = drawn_rows(half_stride)
    twin, twin_which = drawn_rows(half_stride + 1)
    strength = drawn_strength(which)
    twin_strength = drawn_strength(twin_which)
    values = jnp.where(chosen[:, None], strength[:, None] * bases[which], values)
    twin_values = 0.995 * twin_strength[:, None] * bases[twin_which] + 0.3 * noise
    values = jnp.where(twin[:, None], twin_values, values)
    return values.astype(jnp.bfloat16)


def setup_inputs(seed: int = 0) -> dict:
    streams_of = jax.random.split(jax.random.key(seed), 4)
    view_one = draw_view_one(jax.random.fold_in(streams_of[3], 71), 0)
    view_two = draw_view_two(jax.random.fold_in(streams_of[3], 71), 0)
    partner = jax.random.permutation(streams_of[2], USERS).astype(jnp.int32)
    return {"view_one": view_one, "view_two": view_two, "partner": partner}


def reference(view_one, view_two, partner):
    logit_scale = 2.0 / math.sqrt(D)
    block_size = math.gcd(USERS, 512)
    blocks_count = USERS // block_size
    view_blocks = view_one.reshape(blocks_count, block_size, D)
    partner_blocks = partner.reshape(blocks_count, block_size)

    def block_scores(block_rows):
        return logit_scale * jnp.dot(block_rows, view_two.T, preferred_element_type=jnp.float32)

    def stats_step(running, block_rows):
        col_highest, col_total = running
        scores = block_scores(block_rows)
        row_highest = lax.optimization_barrier(jnp.max(scores, axis=1))
        row_lse = row_highest + jnp.log(lax.optimization_barrier(jnp.sum(jnp.exp(scores - row_highest[:, None]), axis=1)))
        new_highest = jnp.maximum(col_highest, lax.optimization_barrier(jnp.max(scores, axis=0)))
        col_total = col_total * jnp.exp(col_highest - new_highest) + lax.optimization_barrier(jnp.sum(jnp.exp(scores - new_highest[None, :]), axis=0))
        return ((new_highest, col_total), row_lse)
    initial = (jnp.full((USERS,), -jnp.inf, jnp.float32), jnp.zeros((USERS,), jnp.float32))
    (col_highest, col_total), row_lses = lax.scan(stats_step, initial, view_blocks)
    col_lse = col_highest + jnp.log(col_total)

    def grad_step(accumulated, inputs):
        block_rows, row_lse, block_partner = inputs
        scores = block_scores(block_rows)
        column_index = lax.broadcasted_iota(jnp.int32, scores.shape, 1)
        positive_mask = (column_index == block_partner[:, None]).astype(jnp.float32)
        coupling = (0.5 * (jnp.exp(scores - row_lse[:, None]) + jnp.exp(scores - col_lse[None, :])) - positive_mask).astype(jnp.bfloat16)
        first_grad = jnp.dot(coupling, view_two, preferred_element_type=jnp.float32)
        accumulated = accumulated + jnp.dot(coupling.T, block_rows, preferred_element_type=jnp.float32)
        return (accumulated, first_grad)
    grad_two, first_blocks = lax.scan(grad_step, jnp.zeros((USERS, D), jnp.float32), (view_blocks, row_lses, partner_blocks))
    grad_one = first_blocks.reshape(USERS, D)
    return (grad_one, grad_two)
```

```python
import functools
import math

import jax
import jax.numpy as jnp
from jax import lax
from jax.experimental import pallas as pl
from jax.experimental.pallas import tpu as pltpu
from jax.sharding import PartitionSpec as P

D = 2048
MESH = pl.DeviceIdType.MESH
NT = (((1,), (1,)), ((), ()))
TN = (((0,), (0,)), ((), ()))


def line_length(users):
    length = 1
    while length * length < users:
        length *= 2
    return length


def kernel(users, feats, one_ref, two_ref, partner_ref, g1_ref, g2_ref,
           views, part, rs, colst, rowst, coup, cols,
           local_sem, view_recv, line_send, group_send, rs_send, rs_recv,
           col_send, col_recv, row_send, row_recv, coup_send, coup_recv,
           turn_send, turn_recv, cols_send, cols_recv):
    rows, width = one_ref.shape
    quarter = rows // feats
    length = line_length(users)
    group = users // length
    scale = 2.0 / math.sqrt(D)
    u = lax.axis_index("user")
    f = lax.axis_index("feat")
    z = u // group
    y = lax.rem(u, group)
    mine = pl.ds(pl.multiple_of(f * quarter, quarter), quarter)

    loads = [pltpu.make_async_copy(ref, views.at[v, u], local_sem.at[v])
             for v, ref in enumerate((two_ref, one_ref))]
    for load in loads:
        load.start()

    def user_at(k):
        return lax.rem(u + k, users)

    def feat_at(k):
        return lax.rem(f + k, feats)

    barrier = pltpu.get_barrier_semaphore()
    for k in range(1, users):
        pl.semaphore_signal(barrier, inc=1, device_id=(user_at(k), f), device_id_type=MESH)
    for k in range(1, feats):
        pl.semaphore_signal(barrier, inc=1, device_id=(u, feat_at(k)), device_id_type=MESH)
    pl.semaphore_wait(barrier, users + feats - 2)

    def remote(src, dst, send, recv, user, feat):
        return pltpu.make_async_remote_copy(
            src_ref=src, dst_ref=dst, send_sem=send, recv_sem=recv,
            device_id=(user, feat), device_id_type=MESH)

    def along(v, b, step):
        return remote(views.at[v, b], views.at[v, b], line_send.at[v, b, (step + 1) // 2],
                      view_recv.at[v, b], u + step * group, f)

    def across(v, b, k):
        return remote(views.at[v, b], views.at[v, b], group_send.at[v, b, k - 1],
                      view_recv.at[v, b], z * group + lax.rem(y + k, group), f)

    def arrived(v, b):
        across(v, b, 1).wait_recv()

    def each_on_line(d, body):
        for step in ((1, -1) if d else (0,)):
            src = z + step * d

            @pl.when((src >= 0) & (src < length))
            def _():
                body(src, step)

    def onward(src, step, act):
        for way in ((-step,) if step else (1, -1)):
            @pl.when((z + way >= 0) & (z + way < length))
            def _():
                act(way)

    def pass_on(v, d):
        def body(src, step):
            b = src * group + y
            if d:
                arrived(v, b)
            onward(src, step, lambda way: along(v, b, way).start())
            for k in range(1, group):
                across(v, b, k).start()
        each_on_line(d, body)

    def sent(v):
        for d in range(length):
            def body(src, step):
                b = src * group + y
                onward(src, step, lambda way: along(v, b, way).wait_send())
                for k in range(1, group):
                    across(v, b, k).wait_send()
            each_on_line(d, body)

    def rs_copy(b, k):
        to = feat_at(k)
        return remote(part.at[b, pl.ds(pl.multiple_of(to * quarter, quarter), quarter)], rs.at[k - 1, b],
                      rs_send.at[k - 1, b], rs_recv.at[k - 1, b], u, to)

    def score(b):
        part[b] = lax.dot_general(views[0, b], views[1, u], NT, preferred_element_type=jnp.float32)
        for k in range(1, feats):
            rs_copy(b, k).start()

    def score_line(d):
        each_on_line(d, lambda src, step: score(src * group + y))

    def score_group(d):
        def body(src, step):
            def one(k, carry):
                b = src * group + lax.rem(y + k, group)
                arrived(0, b)
                score(b)
                return carry
            lax.fori_loop(1, group, one, 0)
        each_on_line(d, body)

    loads[0].wait()
    pass_on(0, 0)
    loads[1].wait()
    score_line(0)
    for d in range(1, length):
        pass_on(0, d)
        score_line(d)
        score_group(d - 1)
    pass_on(1, 0)
    score_group(length - 1)

    def rs_wait(b, carry):
        for k in range(1, feats):
            rs_copy(b, k).wait_recv()
        return carry
    lax.fori_loop(0, users, rs_wait, 0)
    total = part[:, mine, :]
    for k in range(feats - 1):
        total = total + rs[k]
    scores = (scale * total).reshape(users * quarter, rows)
    scores_t = scores.T

    row_high = jnp.max(scores, axis=0, keepdims=True)
    rowst[f, 0:1] = row_high
    rowst[f, 1:2] = jnp.sum(jnp.exp(scores - row_high), axis=0, keepdims=True)
    col_high = jnp.max(scores_t, axis=0, keepdims=True)
    colst[u, 0:1] = col_high
    colst[u, 1:2] = jnp.sum(jnp.exp(scores_t - col_high), axis=0, keepdims=True)

    def col_copy(k):
        return remote(colst.at[u], colst.at[u], col_send.at[k - 1], col_recv.at[k - 1], user_at(k), f)

    def row_copy(k):
        return remote(rowst.at[f], rowst.at[f], row_send.at[k - 1], row_recv.at[k - 1], u, feat_at(k))

    for k in range(1, users):
        col_copy(k).start()
    for k in range(1, feats):
        row_copy(k).start()
    pass_on(1, 1)
    for k in range(1, feats):
        row_copy(k).wait_recv()
    for k in range(1, users):
        col_copy(k).wait_recv()

    def merged(stats, count):
        high = stats[0, 0:1]
        for k in range(1, count):
            high = jnp.maximum(high, stats[k, 0:1])
        whole = jnp.zeros_like(high)
        for k in range(count):
            whole = whole + stats[k, 1:2] * jnp.exp(stats[k, 0:1] - high)
        return high + jnp.log(whole)

    row_lse = merged(rowst, feats)
    col_lse = merged(colst, users)
    both = jnp.exp(scores - row_lse) + jnp.exp(scores_t - col_lse).T
    block = (users, quarter, rows)
    index = (lax.broadcasted_iota(jnp.int32, block, 0) * rows
             + lax.broadcasted_iota(jnp.int32, block, 1) + f * quarter)
    hit = jnp.where(index == partner_ref[...].reshape(1, 1, rows), 1.0, 0.0)
    coupling = (0.5 * both.reshape(block) - hit).astype(jnp.bfloat16)
    coup[:, mine, :] = coupling

    def turn_copy(k):
        return remote(coup.at[user_at(k), mine], cols.at[u, mine],
                      turn_send.at[k - 1], turn_recv.at[k - 1], user_at(k), f)

    def coup_copy(k):
        return remote(coup.at[:, mine], coup.at[:, mine],
                      coup_send.at[k - 1], coup_recv.at[k - 1], u, feat_at(k))

    def cols_copy(k):
        return remote(cols.at[:, mine], cols.at[:, mine],
                      cols_send.at[k - 1], cols_recv.at[k - 1], u, feat_at(k))

    for k in range(1, users):
        turn_copy(k).start()
    for k in range(1, feats):
        coup_copy(k).start()
    cols[u, mine, :] = coup[u, mine, :]
    for d in range(2, length):
        pass_on(1, d)
    for k in range(1, users):
        turn_copy(k).wait_recv()
    for k in range(1, feats):
        cols_copy(k).start()

    def summed(out_ref, term):
        out_ref[...] = term(0)
        if users <= 8:
            for b in range(1, users):
                out_ref[...] += term(b)
        else:
            def step(b, carry):
                out_ref[...] += term(b)
                return carry
            lax.fori_loop(1, users, step, 0)

    for k in range(1, feats):
        coup_copy(k).wait_recv()
    summed(g1_ref, lambda b: lax.dot_general(coup[b], views[0, b], TN, preferred_element_type=jnp.float32))

    for d in range(length):
        def rest(src, step):
            def one(k, carry):
                arrived(1, src * group + lax.rem(y + k, group))
                return carry
            lax.fori_loop(1, group, one, 0)
        each_on_line(d, rest)
    for k in range(1, feats):
        cols_copy(k).wait_recv()
    summed(g2_ref, lambda b: jnp.dot(cols[b], views[1, b], preferred_element_type=jnp.float32))

    sent(0)
    sent(1)

    def rs_sent(b, carry):
        for k in range(1, feats):
            rs_copy(b, k).wait_send()
        return carry
    lax.fori_loop(0, users, rs_sent, 0)
    for k in range(1, users):
        col_copy(k).wait_send()
        turn_copy(k).wait_send()
    for k in range(1, feats):
        row_copy(k).wait_send()
        coup_copy(k).wait_send()
        cols_copy(k).wait_send()


def on_device(users, feats, view_one, view_two, partner):
    rows, width = view_one.shape
    quarter = rows // feats
    group = users // line_length(users)
    out = jax.ShapeDtypeStruct((rows, width), jnp.float32)
    vmem = pl.BlockSpec(memory_space=pltpu.VMEM)
    anywhere = pl.BlockSpec(memory_space=pl.ANY)
    dma = pltpu.SemaphoreType.DMA
    f32, bf16 = jnp.float32, jnp.bfloat16
    return pl.pallas_call(
        functools.partial(kernel, users, feats),
        out_shape=(out, out),
        in_specs=[anywhere, anywhere, vmem],
        out_specs=(vmem, vmem),
        scratch_shapes=[
            pltpu.VMEM((2, users, rows, width), bf16),
            pltpu.VMEM((users, rows, rows), f32),
            pltpu.VMEM((feats - 1, users, quarter, rows), f32),
            pltpu.VMEM((users, 8, users * quarter), f32),
            pltpu.VMEM((feats, 8, rows), f32),
            pltpu.VMEM((users, rows, rows), bf16),
            pltpu.VMEM((users, rows, rows), bf16),
            dma((2,)),
            dma((2, users)),
            dma((2, users, 2)),
            dma((2, users, max(group - 1, 1))),
            dma((feats - 1, users)),
            dma((feats - 1, users)),
            dma((users - 1,)),
            dma((users - 1,)),
            dma((feats - 1,)),
            dma((feats - 1,)),
            dma((feats - 1,)),
            dma((feats - 1,)),
            dma((users - 1,)),
            dma((users - 1,)),
            dma((feats - 1,)),
            dma((feats - 1,)),
        ],
        compiler_params=pltpu.CompilerParams(
            collective_id=0, has_side_effects=True, vmem_limit_bytes=60 * 1024 * 1024),
        cost_estimate=pl.CostEstimate(
            flops=6 * users * rows * rows * width, bytes_accessed=16 * rows * width,
            transcendentals=4 * users * quarter * rows),
    )(view_one, view_two, partner.reshape(1, rows))


def solution(mesh):
    return jax.shard_map(
        functools.partial(on_device, mesh.shape["user"], mesh.shape["feat"]),
        mesh=mesh,
        in_specs=(P("user", "feat"), P("user", "feat"), P("user")),
        out_specs=(P("user", "feat"), P("user", "feat")),
        check_vma=False,
    )
```

```python
import functools
import math

import jax
import jax.numpy as jnp
from jax import lax
from jax.experimental import pallas as pl
from jax.experimental.pallas import tpu as pltpu
from jax.sharding import PartitionSpec as P

D = 2048
MESH = pl.DeviceIdType.MESH
NT = (((1,), (1,)), ((), ()))
TN = (((0,), (0,)), ((), ()))


def line_length(users):
    length = 1
    while length * length < users:
        length *= 2
    return length


def kernel(users, feats, one_ref, two_ref, partner_ref, g1_ref, g2_ref,
           views, partners, part, rs, colst, rowst, stage, coup, cols,
           local_sem, view_recv, line_send, group_send, partner_send, partner_recv,
           rs_send, rs_recv, col_send, col_recv, row_send, row_recv,
           coup_send, coup_recv, turn_send, turn_recv, cols_send, cols_recv):
    rows, width = one_ref.shape
    quarter = rows // feats
    length = line_length(users)
    group = users // length
    plane = group * feats
    scale = 2.0 / math.sqrt(D)
    u = lax.axis_index("user")
    f = lax.axis_index("feat")
    z = u // group
    y = lax.rem(u, group)
    mine = pl.ds(pl.multiple_of(f * quarter, quarter), quarter)

    loads = [pltpu.make_async_copy(ref, views.at[v, u], local_sem.at[v])
             for v, ref in enumerate((two_ref, one_ref))]
    for load in loads:
        load.start()
    partners[y] = partner_ref[...]

    def line_at(k):
        return lax.rem(z + k, length)

    def plane_at(p):
        return lax.rem(y + p // feats, group), lax.rem(f + p % feats, feats)

    barrier = pltpu.get_barrier_semaphore()
    for k in range(1, length):
        pl.semaphore_signal(barrier, inc=1, device_id=(line_at(k) * group + y, f), device_id_type=MESH)
    for p in range(1, plane):
        to_y, to_f = plane_at(p)
        pl.semaphore_signal(barrier, inc=1, device_id=(z * group + to_y, to_f), device_id_type=MESH)
    pl.semaphore_wait(barrier, length + plane - 2)

    def remote(src, dst, send, recv, to_z, to_y, to_f):
        return pltpu.make_async_remote_copy(
            src_ref=src, dst_ref=dst, send_sem=send, recv_sem=recv,
            device_id=(to_z * group + to_y, to_f), device_id_type=MESH)

    def along(v, src, step):
        b = src * group + y
        return remote(views.at[v, b], views.at[v, b], line_send.at[v, src, (step + 1) // 2],
                      view_recv.at[v, b], z + step, y, f)

    def across(v, src, k):
        b = src * group + y
        return remote(views.at[v, b], views.at[v, b], group_send.at[v, src, k - 1],
                      view_recv.at[v, b], z, lax.rem(y + k, group), f)

    def arrived(v, b):
        remote(views.at[v, b], views.at[v, b], line_send.at[v, 0, 0], view_recv.at[v, b], z, y, f).wait_recv()

    def each_on_line(d, body):
        for step in ((1, -1) if d else (0,)):
            src = z + step * d

            @pl.when((src >= 0) & (src < length))
            def _():
                body(src, step)

    def onward(step, act):
        for way in ((-step,) if step else (1, -1)):
            @pl.when((z + way >= 0) & (z + way < length))
            def _():
                act(way)

    def pass_on(v, d):
        def body(src, step):
            if d:
                arrived(v, src * group + y)
            onward(step, lambda way: along(v, src, way).start())
        each_on_line(d, body)

    def cross(v, d):
        def body(src, step):
            for k in range(1, group):
                across(v, src, k).start()
        each_on_line(d, body)

    def sent(v):
        for d in range(length):
            def body(src, step):
                onward(step, lambda way: along(v, src, way).wait_send())
                for k in range(1, group):
                    across(v, src, k).wait_send()
            each_on_line(d, body)

    def crossed(v):
        def one(src, carry):
            for k in range(1, group):
                arrived(v, src * group + lax.rem(y + k, group))
            return carry
        lax.fori_loop(0, length, one, 0)

    def partner_copy(k):
        return remote(partners.at[y], partners.at[y], partner_send.at[k - 1], partner_recv.at[k - 1],
                      z, lax.rem(y + k, group), f)

    def rs_copy(src, k):
        to = lax.rem(f + k, feats)
        return remote(part.at[src, pl.ds(pl.multiple_of(to * quarter, quarter), quarter)], rs.at[k - 1, src],
                      rs_send.at[k - 1, src], rs_recv.at[k - 1, src], z, y, to)

    def score(d):
        def body(src, step):
            part[src] = lax.dot_general(
                views[0, src * group + y], views[1, pl.ds(z * group, group)].reshape(group * rows, width),
                NT, preferred_element_type=jnp.float32)
            for k in range(1, feats):
                rs_copy(src, k).start()
        each_on_line(d, body)

    loads[0].wait()
    pass_on(0, 0)
    loads[1].wait()
    cross(1, 0)
    for k in range(1, group):
        partner_copy(k).start()
    cross(0, 0)
    for k in range(1, group):
        arrived(1, z * group + lax.rem(y + k, group))
    score(0)
    for d in range(1, length):
        pass_on(0, d)
        if d == length - 1:
            pass_on(1, 0)
        score(d)
        cross(0, d)

    def rs_wait(src, carry):
        for k in range(1, feats):
            rs_copy(src, k).wait_recv()
        return carry
    lax.fori_loop(0, length, rs_wait, 0)
    total = part[:, mine, :]
    for k in range(feats - 1):
        total = total + rs[k]
    scores = (scale * total).reshape(length * quarter, group * rows)
    scores_t = scores.T

    row_high = jnp.max(scores, axis=0, keepdims=True)
    row_exp = jnp.exp(scores - row_high)
    rowst[y, f, 0:1] = row_high
    rowst[y, f, 1:2] = jnp.sum(row_exp, axis=0, keepdims=True)
    col_high = jnp.max(scores_t, axis=0, keepdims=True)
    col_exp = jnp.exp(scores_t - col_high)
    colst[z, 0:1] = col_high
    colst[z, 1:2] = jnp.sum(col_exp, axis=0, keepdims=True)

    def col_copy(k):
        return remote(colst.at[z], colst.at[z], col_send.at[k - 1], col_recv.at[k - 1], line_at(k), y, f)

    def row_copy(p):
        return remote(rowst.at[y, f], rowst.at[y, f], row_send.at[p - 1], row_recv.at[p - 1], z, *plane_at(p))

    for k in range(1, length):
        col_copy(k).start()
    for p in range(1, plane):
        row_copy(p).start()
    pass_on(1, 1)
    cross(1, 1)
    for k in range(1, group):
        partner_copy(k).wait_recv()
    for p in range(1, plane):
        row_copy(p).wait_recv()
    for k in range(1, length):
        col_copy(k).wait_recv()

    def share(own, stats):
        high = functools.reduce(jnp.maximum, [highest for highest, _ in stats])
        whole = sum(value * jnp.exp(highest - high) for highest, value in stats)
        return 0.5 * jnp.exp(own - (high + jnp.log(whole)))

    row_share = share(row_high, [(rowst[i, j, 0:1], rowst[i, j, 1:2]) for i in range(group) for j in range(feats)])
    col_share = share(col_high, [(colst[i, 0:1], colst[i, 1:2]) for i in range(length)])
    both = row_exp * row_share + (col_exp * col_share).T
    block = (length, quarter, rows)
    index = (lax.broadcasted_iota(jnp.int32, block, 0) * (group * rows)
             + lax.broadcasted_iota(jnp.int32, block, 1) + (y * rows + f * quarter))
    for i in range(group):
        hit = jnp.where(index == partners[i].reshape(1, 1, rows), 1.0, 0.0)
        stage[i] = (both[:, i * rows:(i + 1) * rows].reshape(block) - hit).astype(jnp.bfloat16)

    def turn_copy(k):
        return remote(stage.at[:, line_at(k)], cols.at[pl.ds(z * group, group), mine],
                      turn_send.at[k - 1], turn_recv.at[k - 1], line_at(k), y, f)

    def coup_copy(p):
        to_y, to_f = plane_at(p)
        return remote(stage.at[to_y], coup.at[:, y, mine], coup_send.at[p - 1], coup_recv.at[p - 1], z, to_y, to_f)

    def cols_copy(k):
        return remote(cols.at[:, mine], cols.at[:, mine],
                      cols_send.at[k - 1], cols_recv.at[k - 1], z, y, lax.rem(f + k, feats))

    for k in range(1, length):
        turn_copy(k).start()
    for p in range(1, plane):
        coup_copy(p).start()
    coup[:, y, mine, :] = stage[y]
    cols[pl.ds(z * group, group), mine, :] = stage[:, z]
    pass_on(1, 2)
    cross(1, 2)
    for k in range(1, length):
        turn_copy(k).wait_recv()
    for k in range(1, feats):
        cols_copy(k).start()
    for d in range(3, length):
        pass_on(1, d)
        cross(1, d)

    def summed(out_ref, term):
        chunk = math.gcd(users, 8)
        out_ref[...] = term(0, chunk)

        def step(c, carry):
            out_ref[...] += term(c * chunk, chunk)
            return carry
        if users > chunk:
            lax.fori_loop(1, users // chunk, step, 0)

    def one_term(b, chunk):
        left = coup[pl.ds(b // group, chunk // group)].reshape(chunk * rows, rows)
        return lax.dot_general(left, views[0, pl.ds(b, chunk)].reshape(chunk * rows, width),
                               TN, preferred_element_type=jnp.float32)

    def two_term(b, chunk):
        left = jnp.concatenate([cols[b + i] for i in range(chunk)], axis=1)
        return jnp.dot(left, views[1, pl.ds(b, chunk)].reshape(chunk * rows, width),
                       preferred_element_type=jnp.float32)

    for p in range(1, plane):
        coup_copy(p).wait_recv()
    crossed(0)
    summed(g1_ref, one_term)

    def late(src, carry):
        @pl.when(src != z)
        def _():
            for k in range(1, group):
                arrived(1, src * group + lax.rem(y + k, group))
        return carry
    lax.fori_loop(0, length, late, 0)
    for k in range(1, feats):
        cols_copy(k).wait_recv()
    summed(g2_ref, two_term)

    sent(0)
    sent(1)

    def rs_sent(src, carry):
        for k in range(1, feats):
            rs_copy(src, k).wait_send()
        return carry
    lax.fori_loop(0, length, rs_sent, 0)
    for k in range(1, group):
        partner_copy(k).wait_send()
    for k in range(1, length):
        col_copy(k).wait_send()
        turn_copy(k).wait_send()
    for p in range(1, plane):
        row_copy(p).wait_send()
        coup_copy(p).wait_send()
    for k in range(1, feats):
        cols_copy(k).wait_send()


def on_device(users, feats, view_one, view_two, partner):
    rows, width = view_one.shape
    quarter = rows // feats
    length = line_length(users)
    group = users // length
    plane = group * feats
    out = jax.ShapeDtypeStruct((rows, width), jnp.float32)
    vmem = pl.BlockSpec(memory_space=pltpu.VMEM)
    anywhere = pl.BlockSpec(memory_space=pl.ANY)
    dma = pltpu.SemaphoreType.DMA
    f32, bf16 = jnp.float32, jnp.bfloat16
    return pl.pallas_call(
        functools.partial(kernel, users, feats),
        out_shape=(out, out),
        in_specs=[anywhere, anywhere, vmem],
        out_specs=(vmem, vmem),
        scratch_shapes=[
            pltpu.VMEM((2, users, rows, width), bf16),
            pltpu.VMEM((group, 1, rows), jnp.int32),
            pltpu.VMEM((length, rows, group * rows), f32),
            pltpu.VMEM((feats - 1, length, quarter, group * rows), f32),
            pltpu.VMEM((length, 8, length * quarter), f32),
            pltpu.VMEM((group, feats, 8, group * rows), f32),
            pltpu.VMEM((group, length, quarter, rows), bf16),
            pltpu.VMEM((length, group, rows, rows), bf16),
            pltpu.VMEM((users, rows, rows), bf16),
            dma((2,)),
            dma((2, users)),
            dma((2, length, 2)),
            dma((2, length, group - 1)),
            dma((group - 1,)), dma((group - 1,)),
            dma((feats - 1, length)), dma((feats - 1, length)),
            dma((length - 1,)), dma((length - 1,)),
            dma((plane - 1,)), dma((plane - 1,)),
            dma((plane - 1,)), dma((plane - 1,)),
            dma((length - 1,)), dma((length - 1,)),
            dma((feats - 1,)), dma((feats - 1,)),
        ],
        compiler_params=pltpu.CompilerParams(
            collective_id=0, has_side_effects=True, vmem_limit_bytes=60 * 1024 * 1024),
        cost_estimate=pl.CostEstimate(
            flops=6 * users * rows * rows * width, bytes_accessed=16 * rows * width,
            transcendentals=4 * users * quarter * rows),
    )(view_one, view_two, partner.reshape(1, rows))


def solution(mesh):
    return jax.shard_map(
        functools.partial(on_device, mesh.shape["user"], mesh.shape["feat"]),
        mesh=mesh,
        in_specs=(P("user", "feat"), P("user", "feat"), P("user")),
        out_specs=(P("user", "feat"), P("user", "feat")),
        check_vma=False,
    )
```

```python
import functools
import math

import jax
import jax.numpy as jnp
from jax import lax
from jax.experimental import pallas as pl
from jax.experimental.pallas import tpu as pltpu
from jax.sharding import PartitionSpec as P

D = 2048
MESH = pl.DeviceIdType.MESH
NT = (((1,), (1,)), ((), ()))
TN = (((0,), (0,)), ((), ()))


def line_length(users):
    length = 1
    while length * length < users:
        length *= 2
    return length


def kernel(users, feats, one_ref, two_ref, partner_ref, g1_ref, g2_ref,
           views, partners, part, rs, colst, rowst, stage, coup, cols,
           local_sem, view_recv, line_send, straight_send, beside_send, group_send, partner_send, partner_recv,
           rs_send, rs_recv, col_send, col_recv, row_send, row_recv,
           coup_send, coup_recv, turn_send, turn_recv, cols_send, cols_recv):
    rows, width = one_ref.shape
    quarter = rows // feats
    length = line_length(users)
    group = users // length
    plane = group * feats
    scale = 2.0 / math.sqrt(D)
    u = lax.axis_index("user")
    f = lax.axis_index("feat")
    z = u // group
    y = lax.rem(u, group)
    mine = pl.ds(pl.multiple_of(f * quarter, quarter), quarter)

    loads = [pltpu.make_async_copy(ref, views.at[v, u], local_sem.at[v])
             for v, ref in enumerate((two_ref, one_ref))]
    loads.append(pltpu.make_async_copy(partner_ref, partners.at[y], local_sem.at[2]))
    for load in loads:
        load.start()

    def line_at(k):
        return lax.rem(z + k, length)

    def plane_at(p):
        return lax.rem(y + p // feats, group), lax.rem(f + p % feats, feats)

    barrier = pltpu.get_barrier_semaphore()
    for k in range(1, length):
        pl.semaphore_signal(barrier, inc=1, device_id=(line_at(k) * group + y, f), device_id_type=MESH)
    for p in range(1, plane):
        to_y, to_f = plane_at(p)
        pl.semaphore_signal(barrier, inc=1, device_id=(z * group + to_y, to_f), device_id_type=MESH)
    pl.semaphore_wait(barrier, length + plane - 2)

    def remote(src, dst, send, recv, to_z, to_y, to_f):
        return pltpu.make_async_remote_copy(
            src_ref=src, dst_ref=dst, send_sem=send, recv_sem=recv,
            device_id=(to_z * group + to_y, to_f), device_id_type=MESH)

    def half(v, b, h):
        return views.at[v, b, pl.ds(h * (rows // 2), rows // 2)]

    def along(src, step, h):
        b = src * group + y
        return remote(half(0, b, h), half(0, b, h), line_send.at[src, (step + 1) // 2, h],
                      view_recv.at[0, b, h], z + step, y, f)

    def straight(k):
        return remote(views.at[1, u], views.at[1, u], straight_send.at[k - 1],
                      view_recv.at[1, u, 0], line_at(k), y, f)

    def beside(step, k):
        b = z * group + lax.rem(y + k, group)
        return remote(views.at[1, b], views.at[1, b], beside_send.at[(step + 1) // 2, k - 1],
                      view_recv.at[1, b, 0], z + step, y, f)

    def across(v, src, k):
        b = src * group + y
        return remote(views.at[v, b], views.at[v, b], group_send.at[v, src, k - 1],
                      view_recv.at[v, b, 0], z, lax.rem(y + k, group), f)

    def arrived(v, b):
        remote(views.at[v, b], views.at[v, b], line_send.at[0, 0, 0], view_recv.at[v, b, 0], z, y, f).wait_recv()

    def each_on_line(d, body):
        for step in ((1, -1) if d else (0,)):
            src = z + step * d

            @pl.when((src >= 0) & (src < length))
            def _():
                body(src, step)

    def onward(step, act):
        for way in ((-step,) if step else (1, -1)):
            @pl.when((z + way >= 0) & (z + way < length))
            def _():
                act(way)

    def pass_on(d):
        for h in range(2):
            def body(src, step):
                if d:
                    along(src, step, h).wait_recv()
                onward(step, lambda way: along(src, way, h).start())
            each_on_line(d, body)

    def first_views():
        for d in range(1, length):
            each_on_line(d, lambda dst, step: straight(d if step > 0 else length - d).start())
        onward(0, lambda way: [beside(way, k).start() for k in range(1, group)])

    def cross(v, d):
        def body(src, step):
            if v and d:
                arrived(1, src * group + y)
            if v == 0 or d != 1:
                for k in range(1, group):
                    across(v, src, k).start()
        each_on_line(d, body)

    def sent():
        for d in range(length):
            def body(src, step):
                for h in range(2):
                    onward(step, lambda way: along(src, way, h).wait_send())
                for v in range(2):
                    if v == 0 or d != 1:
                        for k in range(1, group):
                            across(v, src, k).wait_send()
            each_on_line(d, body)
        for k in range(1, length):
            straight(k).wait_send()
        onward(0, lambda way: [beside(way, k).wait_send() for k in range(1, group)])

    def crossed(v):
        def one(src, carry):
            for k in range(1, group):
                arrived(v, src * group + lax.rem(y + k, group))
            return carry
        lax.fori_loop(0, length, one, 0)

    def partner_copy(k):
        return remote(partners.at[y], partners.at[y], partner_send.at[k - 1], partner_recv.at[k - 1],
                      z, lax.rem(y + k, group), f)

    def rs_copy(src, k):
        to = lax.rem(f + k, feats)
        return remote(part.at[src, pl.ds(pl.multiple_of(to * quarter, quarter), quarter)], rs.at[k - 1, src],
                      rs_send.at[k - 1, src], rs_recv.at[k - 1, src], z, y, to)

    def score(d):
        def body(src, step):
            part[src] = lax.dot_general(
                views[0, src * group + y], views[1, pl.ds(z * group, group)].reshape(group * rows, width),
                NT, preferred_element_type=jnp.float32)
            for k in range(1, feats):
                rs_copy(src, k).start()
        each_on_line(d, body)

    loads[0].wait()
    pass_on(0)
    loads[1].wait()
    cross(1, 0)
    loads[2].wait()
    for k in range(1, group):
        partner_copy(k).start()
    cross(0, 0)
    for k in range(1, group):
        arrived(1, z * group + lax.rem(y + k, group))
    score(0)
    for d in range(1, length):
        pass_on(d)
        if d == max(length - 2, 1):
            first_views()
        score(d)
        cross(0, d)

    def rs_wait(src, carry):
        for k in range(1, feats):
            rs_copy(src, k).wait_recv()
        return carry
    lax.fori_loop(0, length, rs_wait, 0)
    total = part[:, mine, :]
    for k in range(feats - 1):
        total = total + rs[k]
    scores = (scale * total).reshape(length * quarter, group * rows)
    scores_t = scores.T

    row_high = jnp.max(scores, axis=0, keepdims=True)
    row_exp = jnp.exp(scores - row_high)
    rowst[y, f, 0:1] = row_high
    rowst[y, f, 1:2] = jnp.sum(row_exp, axis=0, keepdims=True)
    col_high = jnp.max(scores_t, axis=0, keepdims=True)
    col_exp = jnp.exp(scores_t - col_high)
    colst[z, 0:1] = col_high
    colst[z, 1:2] = jnp.sum(col_exp, axis=0, keepdims=True)

    def col_copy(k):
        return remote(colst.at[z], colst.at[z], col_send.at[k - 1], col_recv.at[k - 1], line_at(k), y, f)

    def row_copy(p):
        return remote(rowst.at[y, f], rowst.at[y, f], row_send.at[p - 1], row_recv.at[p - 1], z, *plane_at(p))

    for k in range(1, length):
        col_copy(k).start()
    for p in range(1, plane):
        row_copy(p).start()
    for k in range(1, group):
        partner_copy(k).wait_recv()
    for p in range(1, plane):
        row_copy(p).wait_recv()
    for k in range(1, length):
        col_copy(k).wait_recv()

    def share(own, stats):
        high = functools.reduce(jnp.maximum, [highest for highest, _ in stats])
        whole = sum(value * jnp.exp(highest - high) for highest, value in stats)
        return 0.5 * jnp.exp(own - (high + jnp.log(whole)))

    row_share = share(row_high, [(rowst[i, j, 0:1], rowst[i, j, 1:2]) for i in range(group) for j in range(feats)])
    col_share = share(col_high, [(colst[i, 0:1], colst[i, 1:2]) for i in range(length)])
    both = row_exp * row_share + (col_exp * col_share).T
    block = (length, quarter, rows)
    index = (lax.broadcasted_iota(jnp.int32, block, 0) * (group * rows)
             + lax.broadcasted_iota(jnp.int32, block, 1) + (y * rows + f * quarter))
    for i in range(group):
        hit = jnp.where(index == partners[i].reshape(1, 1, rows), 1.0, 0.0)
        stage[i] = (both[:, i * rows:(i + 1) * rows].reshape(block) - hit).astype(jnp.bfloat16)

    def turn_copy(k):
        return remote(stage.at[:, line_at(k)], cols.at[pl.ds(z * group, group), mine],
                      turn_send.at[k - 1], turn_recv.at[k - 1], line_at(k), y, f)

    def coup_copy(p):
        to_y, to_f = plane_at(p)
        return remote(stage.at[to_y], coup.at[:, y, mine], coup_send.at[p - 1], coup_recv.at[p - 1], z, to_y, to_f)

    def cols_copy(k):
        return remote(cols.at[:, mine], cols.at[:, mine],
                      cols_send.at[k - 1], cols_recv.at[k - 1], z, y, lax.rem(f + k, feats))

    for k in range(1, length):
        turn_copy(k).start()
    for p in range(1, plane):
        coup_copy(p).start()
    coup[:, y, mine, :] = stage[y]
    cols[pl.ds(z * group, group), mine, :] = stage[:, z]
    for d in range(2, length):
        cross(1, d)
    for k in range(1, length):
        turn_copy(k).wait_recv()
    for k in range(1, feats):
        cols_copy(k).start()

    def summed(out_ref, term):
        chunk = math.gcd(users, 8)
        out_ref[...] = term(0, chunk)

        def step(c, carry):
            out_ref[...] += term(c * chunk, chunk)
            return carry
        if users > chunk:
            lax.fori_loop(1, users // chunk, step, 0)

    def one_term(b, chunk):
        left = coup[pl.ds(b // group, chunk // group)].reshape(chunk * rows, rows)
        return lax.dot_general(left, views[0, pl.ds(b, chunk)].reshape(chunk * rows, width),
                               TN, preferred_element_type=jnp.float32)

    def two_term(b, chunk):
        left = jnp.concatenate([cols[b + i] for i in range(chunk)], axis=1)
        return jnp.dot(left, views[1, pl.ds(b, chunk)].reshape(chunk * rows, width),
                       preferred_element_type=jnp.float32)

    for p in range(1, plane):
        coup_copy(p).wait_recv()
    crossed(0)
    summed(g1_ref, one_term)

    cross(1, 1)

    def late(src, carry):
        @pl.when(src != z)
        def _():
            for k in range(1, group):
                arrived(1, src * group + lax.rem(y + k, group))
        return carry
    lax.fori_loop(0, length, late, 0)
    for k in range(1, feats):
        cols_copy(k).wait_recv()
    summed(g2_ref, two_term)

    sent()

    def rs_sent(src, carry):
        for k in range(1, feats):
            rs_copy(src, k).wait_send()
        return carry
    lax.fori_loop(0, length, rs_sent, 0)
    for k in range(1, group):
        partner_copy(k).wait_send()
    for k in range(1, length):
        col_copy(k).wait_send()
        turn_copy(k).wait_send()
    for p in range(1, plane):
        row_copy(p).wait_send()
        coup_copy(p).wait_send()
    for k in range(1, feats):
        cols_copy(k).wait_send()


def hand_out(one_ref, two_ref, one_out, two_out, sems):
    copies = [pltpu.make_async_copy(one_ref, one_out, sems.at[0]),
              pltpu.make_async_copy(two_ref, two_out, sems.at[1])]
    for copy in copies:
        copy.start()
    for copy in copies:
        copy.wait()


def on_device(users, feats, view_one, view_two, partner):
    rows, width = view_one.shape
    quarter = rows // feats
    length = line_length(users)
    group = users // length
    plane = group * feats
    out = jax.ShapeDtypeStruct((rows, width), jnp.float32)
    vmem = pl.BlockSpec(memory_space=pltpu.VMEM)
    anywhere = pl.BlockSpec(memory_space=pl.ANY)
    dma = pltpu.SemaphoreType.DMA
    f32, bf16 = jnp.float32, jnp.bfloat16
    grads = pl.pallas_call(
        functools.partial(kernel, users, feats),
        out_shape=(out, out),
        in_specs=[pl.BlockSpec(memory_space=pltpu.HBM)] * 3,
        out_specs=(vmem, vmem),
        scratch_shapes=[
            pltpu.VMEM((2, users, rows, width), bf16),
            pltpu.VMEM((group, 1, rows), jnp.int32),
            pltpu.VMEM((length, rows, group * rows), f32),
            pltpu.VMEM((feats - 1, length, quarter, group * rows), f32),
            pltpu.VMEM((length, 8, length * quarter), f32),
            pltpu.VMEM((group, feats, 8, group * rows), f32),
            pltpu.VMEM((group, length, quarter, rows), bf16),
            pltpu.VMEM((length, group, rows, rows), bf16),
            pltpu.VMEM((users, rows, rows), bf16),
            dma((3,)),
            dma((2, users, 2)),
            dma((length, 2, 2)),
            dma((length - 1,)),
            dma((2, group - 1)),
            dma((2, length, group - 1)),
            dma((group - 1,)), dma((group - 1,)),
            dma((feats - 1, length)), dma((feats - 1, length)),
            dma((length - 1,)), dma((length - 1,)),
            dma((plane - 1,)), dma((plane - 1,)),
            dma((plane - 1,)), dma((plane - 1,)),
            dma((length - 1,)), dma((length - 1,)),
            dma((feats - 1,)), dma((feats - 1,)),
        ],
        compiler_params=pltpu.CompilerParams(
            collective_id=0, has_side_effects=True, vmem_limit_bytes=min(60, 8 + users) * 1024 * 1024),
        cost_estimate=pl.CostEstimate(
            flops=6 * users * rows * rows * width, bytes_accessed=16 * rows * width,
            transcendentals=4 * users * quarter * rows),
    )(view_one, view_two, partner.reshape(1, rows))
    return pl.pallas_call(
        hand_out,
        out_shape=(out, out),
        in_specs=[anywhere, anywhere],
        out_specs=(anywhere, anywhere),
        scratch_shapes=[dma((2,))],
    )(*grads)


def solution(mesh):
    return jax.shard_map(
        functools.partial(on_device, mesh.shape["user"], mesh.shape["feat"]),
        mesh=mesh,
        in_specs=(P("user", "feat"), P("user", "feat"), P("user")),
        out_specs=(P("user", "feat"), P("user", "feat")),
        check_vma=False,
    )
```

```python
import functools
import math

import jax
import jax.numpy as jnp
from jax import lax
from jax.experimental import pallas as pl
from jax.experimental.pallas import tpu as pltpu
from jax.sharding import PartitionSpec as P

D = 2048
VMEM_BYTES = 60 * 1024 * 1024
MESH = pl.DeviceIdType.MESH
NT = (((1,), (1,)), ((), ()))
TN = (((0,), (0,)), ((), ()))


def line_length(users):
    length = 1
    while length * length < users:
        length *= 2
    return length


def kernel(users, feats, one_ref, two_ref, partner_ref, g1_ref, g2_ref,
           views, partners, part, rs, colst, rowst, stage, coup, cols,
           local_sem, view_recv, line_send, straight_send, beside_send, group_send, partner_send, partner_recv,
           rs_send, rs_recv, col_send, col_recv, row_send, row_recv,
           coup_send, coup_recv, turn_send, turn_recv, cols_send, cols_recv):
    rows, width = one_ref.shape
    quarter = rows // feats
    length = line_length(users)
    group = users // length
    plane = group * feats
    scale = 2.0 / math.sqrt(D)
    u = lax.axis_index("user")
    f = lax.axis_index("feat")
    z = u // group
    y = lax.rem(u, group)
    mine = pl.ds(pl.multiple_of(f * quarter, quarter), quarter)

    loads = [pltpu.make_async_copy(ref, views.at[v, u], local_sem.at[v])
             for v, ref in enumerate((two_ref, one_ref))]
    loads.append(pltpu.make_async_copy(partner_ref, partners.at[y], local_sem.at[2]))
    for load in loads:
        load.start()

    def line_at(k):
        return lax.rem(z + k, length)

    def plane_at(p):
        return lax.rem(y + p // feats, group), lax.rem(f + p % feats, feats)

    barrier = pltpu.get_barrier_semaphore()
    for k in range(1, length):
        pl.semaphore_signal(barrier, inc=1, device_id=(line_at(k) * group + y, f), device_id_type=MESH)
    for p in range(1, plane):
        to_y, to_f = plane_at(p)
        pl.semaphore_signal(barrier, inc=1, device_id=(z * group + to_y, to_f), device_id_type=MESH)
    pl.semaphore_wait(barrier, length + plane - 2)

    def remote(src, dst, send, recv, to_z, to_y, to_f):
        return pltpu.make_async_remote_copy(
            src_ref=src, dst_ref=dst, send_sem=send, recv_sem=recv,
            device_id=(to_z * group + to_y, to_f), device_id_type=MESH)

    def half(v, b, h):
        return views.at[v, b, pl.ds(h * (rows // 2), rows // 2)]

    def along(src, step, h):
        b = src * group + y
        return remote(half(0, b, h), half(0, b, h), line_send.at[src, (step + 1) // 2, h],
                      view_recv.at[0, b, h], z + step, y, f)

    def straight(v, k):
        return remote(views.at[v, u], views.at[v, u], straight_send.at[v, k - 1],
                      view_recv.at[v, u, 0], line_at(k), y, f)

    def beside(step, k):
        b = z * group + lax.rem(y + k, group)
        return remote(views.at[1, b], views.at[1, b], beside_send.at[(step + 1) // 2, k - 1],
                      view_recv.at[1, b, 0], z + step, y, f)

    def across(v, src, k):
        b = src * group + y
        return remote(views.at[v, b], views.at[v, b], group_send.at[v, src, k - 1],
                      view_recv.at[v, b, 0], z, lax.rem(y + k, group), f)

    def arrived(v, b):
        remote(views.at[v, b], views.at[v, b], line_send.at[0, 0, 0], view_recv.at[v, b, 0], z, y, f).wait_recv()

    def each_on_line(d, body):
        for step in ((1, -1) if d else (0,)):
            src = z + step * d

            @pl.when((src >= 0) & (src < length))
            def _():
                body(src, step)

    def onward(step, act):
        for way in ((-step,) if step else (1, -1)):
            @pl.when((z + way >= 0) & (z + way < length))
            def _():
                act(way)

    def far(v, d, act):
        each_on_line(d, lambda dst, step: act(straight(v, d if step > 0 else length - d)))

    def pass_on(d):
        for h in range(2):
            def body(src, step):
                if d:
                    along(src, step, h).wait_recv()
                if d < 2:
                    onward(step, lambda way: along(src, way, h).start())
            if d < 3:
                each_on_line(d, body)
        if d == 0:
            for reach in range(length - 1, 2, -1):
                far(0, reach, lambda copy: copy.start())
        if d > 2:
            each_on_line(d, lambda src, step: arrived(0, src * group + y))

    def first_views():
        for d in range(length - 1, 0, -1):
            far(1, d, lambda copy: copy.start())
        onward(0, lambda way: [beside(way, k).start() for k in range(1, group)])

    def cross(v, d):
        def body(src, step):
            if v and d:
                arrived(1, src * group + y)
            if v == 0 or d != 1:
                for k in range(1, group):
                    across(v, src, k).start()
        each_on_line(d, body)

    def sent():
        for d in range(length):
            def body(src, step):
                for h in range(2 if d < 2 else 0):
                    onward(step, lambda way: along(src, way, h).wait_send())
                for v in range(2):
                    if v == 0 or d != 1:
                        for k in range(1, group):
                            across(v, src, k).wait_send()
            each_on_line(d, body)
        for d in range(1, length):
            far(1, d, lambda copy: copy.wait_send())
        for d in range(3, length):
            far(0, d, lambda copy: copy.wait_send())
        onward(0, lambda way: [beside(way, k).wait_send() for k in range(1, group)])

    def crossed(v):
        def one(src, carry):
            for k in range(1, group):
                arrived(v, src * group + lax.rem(y + k, group))
            return carry
        lax.fori_loop(0, length, one, 0)

    def partner_copy(k):
        return remote(partners.at[y], partners.at[y], partner_send.at[k - 1], partner_recv.at[k - 1],
                      z, lax.rem(y + k, group), f)

    def rs_copy(src, k):
        to = lax.rem(f + k, feats)
        return remote(part.at[src, pl.ds(pl.multiple_of(to * quarter, quarter), quarter)], rs.at[k - 1, src],
                      rs_send.at[k - 1, src], rs_recv.at[k - 1, src], z, y, to)

    def score(d):
        def body(src, step):
            part[src] = lax.dot_general(
                views[0, src * group + y], views[1, pl.ds(z * group, group)].reshape(group * rows, width),
                NT, preferred_element_type=jnp.float32)
            for k in range(1, feats):
                rs_copy(src, k).start()
        each_on_line(d, body)

    loads[0].wait()
    pass_on(0)
    loads[1].wait()
    cross(1, 0)
    loads[2].wait()
    for k in range(1, group):
        partner_copy(k).start()
    cross(0, 0)
    for k in range(1, group):
        arrived(1, z * group + lax.rem(y + k, group))
    score(0)
    for d in range(1, length):
        pass_on(d)
        if d == 1:
            first_views()
        score(d)
        cross(0, d)

    def rs_wait(src, carry):
        for k in range(1, feats):
            rs_copy(src, k).wait_recv()
        return carry
    lax.fori_loop(0, length, rs_wait, 0)
    total = part[:, mine, :]
    for k in range(feats - 1):
        total = total + rs[k]
    scores = (scale * total).reshape(length * quarter, group * rows)
    scores_t = scores.T

    row_high = jnp.max(scores, axis=0, keepdims=True)
    row_exp = jnp.exp(scores - row_high)
    rowst[y, f, 0:1] = row_high
    rowst[y, f, 1:2] = jnp.sum(row_exp, axis=0, keepdims=True)
    col_high = jnp.max(scores_t, axis=0, keepdims=True)
    col_exp = jnp.exp(scores_t - col_high)
    colst[z, 0:1] = col_high
    colst[z, 1:2] = jnp.sum(col_exp, axis=0, keepdims=True)

    def col_copy(k):
        return remote(colst.at[z], colst.at[z], col_send.at[k - 1], col_recv.at[k - 1], line_at(k), y, f)

    def row_copy(p):
        return remote(rowst.at[y, f], rowst.at[y, f], row_send.at[p - 1], row_recv.at[p - 1], z, *plane_at(p))

    for k in range(1, length):
        col_copy(k).start()
    for p in range(1, plane):
        row_copy(p).start()
    for k in range(1, group):
        partner_copy(k).wait_recv()
    for p in range(1, plane):
        row_copy(p).wait_recv()
    for k in range(1, length):
        col_copy(k).wait_recv()

    def share(own, stats):
        high = functools.reduce(jnp.maximum, [highest for highest, _ in stats])
        whole = sum(value * jnp.exp(highest - high) for highest, value in stats)
        return 0.5 * jnp.exp(own - (high + jnp.log(whole)))

    row_share = share(row_high, [(rowst[i, j, 0:1], rowst[i, j, 1:2]) for i in range(group) for j in range(feats)])
    col_share = share(col_high, [(colst[i, 0:1], colst[i, 1:2]) for i in range(length)])
    both = row_exp * row_share + (col_exp * col_share).T
    block = (length, quarter, rows)
    index = (lax.broadcasted_iota(jnp.int32, block, 0) * (group * rows)
             + lax.broadcasted_iota(jnp.int32, block, 1) + (y * rows + f * quarter))
    for i in range(group):
        hit = jnp.where(index == partners[i].reshape(1, 1, rows), 1.0, 0.0)
        stage[i] = (both[:, i * rows:(i + 1) * rows].reshape(block) - hit).astype(jnp.bfloat16)

    def turn_copy(k):
        return remote(stage.at[:, line_at(k)], cols.at[pl.ds(z * group, group), mine],
                      turn_send.at[k - 1], turn_recv.at[k - 1], line_at(k), y, f)

    def coup_copy(p):
        to_y, to_f = plane_at(p)
        return remote(stage.at[to_y], coup.at[:, y, mine], coup_send.at[p - 1], coup_recv.at[p - 1], z, to_y, to_f)

    def cols_copy(k):
        return remote(cols.at[:, mine], cols.at[:, mine],
                      cols_send.at[k - 1], cols_recv.at[k - 1], z, y, lax.rem(f + k, feats))

    for k in range(1, length):
        turn_copy(k).start()
    for p in range(1, plane):
        coup_copy(p).start()
    coup[:, y, mine, :] = stage[y]
    cols[pl.ds(z * group, group), mine, :] = stage[:, z]
    for d in range(2, length):
        cross(1, d)
    for k in range(1, length):
        turn_copy(k).wait_recv()
    for k in range(1, feats):
        cols_copy(k).start()

    def summed(out_ref, term):
        chunk = math.gcd(users, 8)
        out_ref[...] = term(0, chunk)

        def step(c, carry):
            out_ref[...] += term(c * chunk, chunk)
            return carry
        if users > chunk:
            lax.fori_loop(1, users // chunk, step, 0)

    def one_term(b, chunk):
        left = coup[pl.ds(b // group, chunk // group)].reshape(chunk * rows, rows)
        return lax.dot_general(left, views[0, pl.ds(b, chunk)].reshape(chunk * rows, width),
                               TN, preferred_element_type=jnp.float32)

    def two_term(b, chunk):
        left = jnp.concatenate([cols[b + i] for i in range(chunk)], axis=1)
        return jnp.dot(left, views[1, pl.ds(b, chunk)].reshape(chunk * rows, width),
                       preferred_element_type=jnp.float32)

    for p in range(1, plane):
        coup_copy(p).wait_recv()
    crossed(0)
    summed(g1_ref, one_term)

    cross(1, 1)

    def late(src, carry):
        @pl.when(src != z)
        def _():
            for k in range(1, group):
                arrived(1, src * group + lax.rem(y + k, group))
        return carry
    lax.fori_loop(0, length, late, 0)
    for k in range(1, feats):
        cols_copy(k).wait_recv()
    summed(g2_ref, two_term)

    sent()

    def rs_sent(src, carry):
        for k in range(1, feats):
            rs_copy(src, k).wait_send()
        return carry
    lax.fori_loop(0, length, rs_sent, 0)
    for k in range(1, group):
        partner_copy(k).wait_send()
    for k in range(1, length):
        col_copy(k).wait_send()
        turn_copy(k).wait_send()
    for p in range(1, plane):
        row_copy(p).wait_send()
        coup_copy(p).wait_send()
    for k in range(1, feats):
        cols_copy(k).wait_send()


def hand_out(one_ref, two_ref, one_out, two_out, held, come, go):
    rows = held.shape[1] // 2
    parts = [(v, h, ref.at[pl.ds(h * rows, rows)], out.at[pl.ds(h * rows, rows)], held.at[v, pl.ds(h * rows, rows)])
             for v, (ref, out) in enumerate(((one_ref, one_out), (two_ref, two_out))) for h in range(2)]
    ins = [pltpu.make_async_copy(src, slot, come.at[v, h]) for v, h, src, _, slot in parts]
    outs = [pltpu.make_async_copy(slot, dst, go.at[v, h]) for v, h, _, dst, slot in parts]
    for copy in ins:
        copy.start()
    for copy, out in zip(ins, outs):
        copy.wait()
        out.start()
    for out in outs:
        out.wait()


def on_device(users, feats, view_one, view_two, partner):
    rows, width = view_one.shape
    quarter = rows // feats
    length = line_length(users)
    group = users // length
    plane = group * feats
    out = jax.ShapeDtypeStruct((rows, width), jnp.float32)
    vmem = pl.BlockSpec(memory_space=pltpu.VMEM)
    anywhere = pl.BlockSpec(memory_space=pl.ANY)
    dma = pltpu.SemaphoreType.DMA
    f32, bf16 = jnp.float32, jnp.bfloat16
    grads = pl.pallas_call(
        functools.partial(kernel, users, feats),
        out_shape=(out, out),
        in_specs=[anywhere] * 3,
        out_specs=(vmem, vmem),
        scratch_shapes=[
            pltpu.VMEM((2, users, rows, width), bf16),
            pltpu.VMEM((group, 1, rows), jnp.int32),
            pltpu.VMEM((length, rows, group * rows), f32),
            pltpu.VMEM((feats - 1, length, quarter, group * rows), f32),
            pltpu.VMEM((length, 8, length * quarter), f32),
            pltpu.VMEM((group, feats, 8, group * rows), f32),
            pltpu.VMEM((group, length, quarter, rows), bf16),
            pltpu.VMEM((length, group, rows, rows), bf16),
            pltpu.VMEM((users, rows, rows), bf16),
            dma((3,)),
            dma((2, users, 2)),
            dma((length, 2, 2)),
            dma((2, length - 1)),
            dma((2, group - 1)),
            dma((2, length, group - 1)),
            dma((group - 1,)), dma((group - 1,)),
            dma((feats - 1, length)), dma((feats - 1, length)),
            dma((length - 1,)), dma((length - 1,)),
            dma((plane - 1,)), dma((plane - 1,)),
            dma((plane - 1,)), dma((plane - 1,)),
            dma((length - 1,)), dma((length - 1,)),
            dma((feats - 1,)), dma((feats - 1,)),
        ],
        compiler_params=pltpu.CompilerParams(
            collective_id=0, has_side_effects=True, vmem_limit_bytes=VMEM_BYTES),
        cost_estimate=pl.CostEstimate(
            flops=6 * users * rows * rows * width, bytes_accessed=16 * rows * width,
            transcendentals=4 * users * quarter * rows),
    )(view_one, view_two, partner.reshape(1, rows))
    return pl.pallas_call(
        hand_out,
        out_shape=(out, out),
        in_specs=[anywhere, anywhere],
        out_specs=(anywhere, anywhere),
        scratch_shapes=[pltpu.VMEM((2, rows, width), f32), dma((2, 2)), dma((2, 2))],
        compiler_params=pltpu.CompilerParams(vmem_limit_bytes=VMEM_BYTES),
    )(*grads)


def solution(mesh):
    return jax.shard_map(
        functools.partial(on_device, mesh.shape["user"], mesh.shape["feat"]),
        mesh=mesh,
        in_specs=(P("user", "feat"), P("user", "feat"), P("user")),
        out_specs=(P("user", "feat"), P("user", "feat")),
        check_vma=False,
    )
```

```python
import functools
import math

import jax
import jax.numpy as jnp
from jax import lax
from jax.experimental import pallas as pl
from jax.experimental.pallas import tpu as pltpu
from jax.sharding import PartitionSpec as P

D = 2048
VMEM_BYTES = 60 * 1024 * 1024
MESH = pl.DeviceIdType.MESH
NT = (((1,), (1,)), ((), ()))
TN = (((0,), (0,)), ((), ()))


def line_length(users):
    length = 1
    while length * length < users:
        length *= 2
    return length


def kernel(users, feats, one_ref, two_ref, partner_ref, g1_ref, g2_ref,
           views, partners, part, rs, colst, rowst, stage, coup, cols,
           local_sem, view_recv, line_send, straight_send, group_send, partner_send, partner_recv,
           rs_send, rs_recv, col_send, col_recv, row_send, row_recv,
           coup_send, coup_recv, turn_send, turn_recv, cols_send, cols_recv):
    rows, width = one_ref.shape
    quarter = rows // feats
    length = line_length(users)
    group = users // length
    plane = group * feats
    scale = 2.0 / math.sqrt(D)
    u = lax.axis_index("user")
    f = lax.axis_index("feat")
    z = u // group
    y = lax.rem(u, group)
    mine = pl.ds(pl.multiple_of(f * quarter, quarter), quarter)

    loads = [pltpu.make_async_copy(ref, views.at[v, u], local_sem.at[v])
             for v, ref in enumerate((two_ref, one_ref))]
    loads.append(pltpu.make_async_copy(partner_ref, partners.at[y], local_sem.at[2]))
    for load in loads:
        load.start()

    def line_at(k):
        return lax.rem(z + k, length)

    def plane_at(p):
        return lax.rem(y + p // feats, group), lax.rem(f + p % feats, feats)

    barrier = pltpu.get_barrier_semaphore()
    for k in range(1, length):
        pl.semaphore_signal(barrier, inc=1, device_id=(line_at(k) * group + y, f), device_id_type=MESH)
    for p in range(1, plane):
        to_y, to_f = plane_at(p)
        pl.semaphore_signal(barrier, inc=1, device_id=(z * group + to_y, to_f), device_id_type=MESH)
    pl.semaphore_wait(barrier, length + plane - 2)

    def remote(src, dst, send, recv, to_z, to_y, to_f):
        return pltpu.make_async_remote_copy(
            src_ref=src, dst_ref=dst, send_sem=send, recv_sem=recv,
            device_id=(to_z * group + to_y, to_f), device_id_type=MESH)

    def half(v, b, h):
        return views.at[v, b, pl.ds(h * (rows // 2), rows // 2)]

    def along(src, step, h):
        b = src * group + y
        return remote(half(0, b, h), half(0, b, h), line_send.at[src, (step + 1) // 2, h],
                      view_recv.at[0, b, h], z + step, y, f)

    def straight(v, k):
        return remote(views.at[v, u], views.at[v, u], straight_send.at[v, k - 1],
                      view_recv.at[v, u, 0], line_at(k), y, f)

    def across(v, src, k):
        b = src * group + y
        return remote(views.at[v, b], views.at[v, b], group_send.at[v, src, k - 1],
                      view_recv.at[v, b, 0], z, lax.rem(y + k, group), f)

    def arrived(v, b):
        remote(views.at[v, b], views.at[v, b], line_send.at[0, 0, 0], view_recv.at[v, b, 0], z, y, f).wait_recv()

    def each_on_line(d, body):
        for step in ((1, -1) if d else (0,)):
            src = z + step * d

            @pl.when((src >= 0) & (src < length))
            def _():
                body(src, step)

    def onward(step, act):
        for way in ((-step,) if step else (1, -1)):
            @pl.when((z + way >= 0) & (z + way < length))
            def _():
                act(way)

    def far(v, d, act):
        each_on_line(d, lambda dst, step: act(straight(v, d if step > 0 else length - d)))

    def pass_on(d):
        for h in range(2):
            def body(src, step):
                if d:
                    along(src, step, h).wait_recv()
                if d < 2:
                    onward(step, lambda way: along(src, way, h).start())
            if d < 3:
                each_on_line(d, body)
        if d == 0:
            for reach in range(length - 1, 2, -1):
                far(0, reach, lambda copy: copy.start())
        if d > 2:
            each_on_line(d, lambda src, step: arrived(0, src * group + y))

    def cross(v, d):
        def body(src, step):
            if v and d:
                arrived(1, src * group + y)
            for k in range(1, group):
                across(v, src, k).start()
        each_on_line(d, body)

    def sent():
        for d in range(length):
            def body(src, step):
                for h in range(2 if d < 2 else 0):
                    onward(step, lambda way: along(src, way, h).wait_send())
                for v in range(2):
                    for k in range(1, group):
                        across(v, src, k).wait_send()
            each_on_line(d, body)
        for d in range(1, length):
            far(1, d, lambda copy: copy.wait_send())
        for d in range(3, length):
            far(0, d, lambda copy: copy.wait_send())

    def crossed(v):
        def one(src, carry):
            for k in range(1, group):
                arrived(v, src * group + lax.rem(y + k, group))
            return carry
        lax.fori_loop(0, length, one, 0)

    def partner_copy(k):
        return remote(partners.at[y], partners.at[y], partner_send.at[k - 1], partner_recv.at[k - 1],
                      z, lax.rem(y + k, group), f)

    def rs_copy(src, k):
        to = lax.rem(f + k, feats)
        return remote(part.at[src, pl.ds(pl.multiple_of(to * quarter, quarter), quarter)], rs.at[k - 1, src],
                      rs_send.at[k - 1, src], rs_recv.at[k - 1, src], z, y, to)

    def score(d):
        def body(src, step):
            part[src] = lax.dot_general(
                views[0, src * group + y], views[1, pl.ds(z * group, group)].reshape(group * rows, width),
                NT, preferred_element_type=jnp.float32)
            for k in range(1, feats):
                rs_copy(src, k).start()
        each_on_line(d, body)

    loads[0].wait()
    pass_on(0)
    loads[1].wait()
    cross(1, 0)
    loads[2].wait()
    for k in range(1, group):
        partner_copy(k).start()
    cross(0, 0)
    for k in range(1, group):
        arrived(1, z * group + lax.rem(y + k, group))
    score(0)
    for d in range(1, length):
        pass_on(d)
        if d == length - 1:
            for reach in range(1, length):
                far(1, reach, lambda copy: copy.start())
        score(d)
        cross(0, d)

    def rs_wait(src, carry):
        for k in range(1, feats):
            rs_copy(src, k).wait_recv()
        return carry
    lax.fori_loop(0, length, rs_wait, 0)
    total = part[:, mine, :]
    for k in range(feats - 1):
        total = total + rs[k]
    scores = (scale * total).reshape(length * quarter, group * rows)
    scores_t = scores.T

    row_high = jnp.max(scores, axis=0, keepdims=True)
    row_exp = jnp.exp(scores - row_high)
    rowst[y, f, 0:1] = row_high
    rowst[y, f, 1:2] = jnp.sum(row_exp, axis=0, keepdims=True)
    col_high = jnp.max(scores_t, axis=0, keepdims=True)
    col_exp = jnp.exp(scores_t - col_high)
    colst[z, 0:1] = col_high
    colst[z, 1:2] = jnp.sum(col_exp, axis=0, keepdims=True)

    def col_copy(k):
        return remote(colst.at[z], colst.at[z], col_send.at[k - 1], col_recv.at[k - 1], line_at(k), y, f)

    def row_copy(p):
        return remote(rowst.at[y, f], rowst.at[y, f], row_send.at[p - 1], row_recv.at[p - 1], z, *plane_at(p))

    for k in range(1, length):
        col_copy(k).start()
    for p in range(1, plane):
        row_copy(p).start()
    cross(1, 1)
    for k in range(1, group):
        partner_copy(k).wait_recv()
    for p in range(1, plane):
        row_copy(p).wait_recv()
    for k in range(1, length):
        col_copy(k).wait_recv()

    def share(own, stats):
        high = functools.reduce(jnp.maximum, [highest for highest, _ in stats])
        whole = sum(value * jnp.exp(highest - high) for highest, value in stats)
        return 0.5 * jnp.exp(own - (high + jnp.log(whole)))

    row_share = share(row_high, [(rowst[i, j, 0:1], rowst[i, j, 1:2]) for i in range(group) for j in range(feats)])
    col_share = share(col_high, [(colst[i, 0:1], colst[i, 1:2]) for i in range(length)])
    both = row_exp * row_share + (col_exp * col_share).T
    block = (length, quarter, rows)
    index = (lax.broadcasted_iota(jnp.int32, block, 0) * (group * rows)
             + lax.broadcasted_iota(jnp.int32, block, 1) + (y * rows + f * quarter))
    for i in range(group):
        hit = jnp.where(index == partners[i].reshape(1, 1, rows), 1.0, 0.0)
        stage[i] = (both[:, i * rows:(i + 1) * rows].reshape(block) - hit).astype(jnp.bfloat16)

    def turn_copy(k):
        return remote(stage.at[:, line_at(k)], cols.at[pl.ds(z * group, group), mine],
                      turn_send.at[k - 1], turn_recv.at[k - 1], line_at(k), y, f)

    def coup_copy(p):
        to_y, to_f = plane_at(p)
        return remote(stage.at[to_y], coup.at[:, y, mine], coup_send.at[p - 1], coup_recv.at[p - 1], z, to_y, to_f)

    def cols_copy(k):
        return remote(cols.at[:, mine], cols.at[:, mine],
                      cols_send.at[k - 1], cols_recv.at[k - 1], z, y, lax.rem(f + k, feats))

    for k in range(1, length):
        turn_copy(k).start()
    for p in range(1, plane):
        coup_copy(p).start()
    coup[:, y, mine, :] = stage[y]
    cols[pl.ds(z * group, group), mine, :] = stage[:, z]
    cross(1, 2)
    for k in range(1, length):
        turn_copy(k).wait_recv()
    for k in range(1, feats):
        cols_copy(k).start()
    for d in range(3, length):
        cross(1, d)

    def summed(out_ref, term):
        chunk = math.gcd(users, 8)
        out_ref[...] = term(0, chunk)

        def step(c, carry):
            out_ref[...] += term(c * chunk, chunk)
            return carry
        if users > chunk:
            lax.fori_loop(1, users // chunk, step, 0)

    def one_term(b, chunk):
        left = coup[pl.ds(b // group, chunk // group)].reshape(chunk * rows, rows)
        return lax.dot_general(left, views[0, pl.ds(b, chunk)].reshape(chunk * rows, width),
                               TN, preferred_element_type=jnp.float32)

    def two_term(b, chunk):
        left = jnp.concatenate([cols[b + i] for i in range(chunk)], axis=1)
        return jnp.dot(left, views[1, pl.ds(b, chunk)].reshape(chunk * rows, width),
                       preferred_element_type=jnp.float32)

    for p in range(1, plane):
        coup_copy(p).wait_recv()
    crossed(0)
    summed(g1_ref, one_term)

    def late(src, carry):
        @pl.when(src != z)
        def _():
            for k in range(1, group):
                arrived(1, src * group + lax.rem(y + k, group))
        return carry
    lax.fori_loop(0, length, late, 0)
    for k in range(1, feats):
        cols_copy(k).wait_recv()
    summed(g2_ref, two_term)

    sent()

    def rs_sent(src, carry):
        for k in range(1, feats):
            rs_copy(src, k).wait_send()
        return carry
    lax.fori_loop(0, length, rs_sent, 0)
    for k in range(1, group):
        partner_copy(k).wait_send()
    for k in range(1, length):
        col_copy(k).wait_send()
        turn_copy(k).wait_send()
    for p in range(1, plane):
        row_copy(p).wait_send()
        coup_copy(p).wait_send()
    for k in range(1, feats):
        cols_copy(k).wait_send()


def hand_out(one_ref, two_ref, one_out, two_out, held, come, go):
    rows = held.shape[1] // 2
    parts = [(v, h, ref.at[pl.ds(h * rows, rows)], out.at[pl.ds(h * rows, rows)], held.at[v, pl.ds(h * rows, rows)])
             for v, (ref, out) in enumerate(((one_ref, one_out), (two_ref, two_out))) for h in range(2)]
    ins = [pltpu.make_async_copy(src, slot, come.at[v, h]) for v, h, src, _, slot in parts]
    outs = [pltpu.make_async_copy(slot, dst, go.at[v, h]) for v, h, _, dst, slot in parts]
    for copy in ins:
        copy.start()
    for copy, out in zip(ins, outs):
        copy.wait()
        out.start()
    for out in outs:
        out.wait()


def on_device(users, feats, view_one, view_two, partner):
    rows, width = view_one.shape
    quarter = rows // feats
    length = line_length(users)
    group = users // length
    plane = group * feats
    out = jax.ShapeDtypeStruct((rows, width), jnp.float32)
    vmem = pl.BlockSpec(memory_space=pltpu.VMEM)
    anywhere = pl.BlockSpec(memory_space=pl.ANY)
    dma = pltpu.SemaphoreType.DMA
    f32, bf16 = jnp.float32, jnp.bfloat16
    grads = pl.pallas_call(
        functools.partial(kernel, users, feats),
        out_shape=(out, out),
        in_specs=[anywhere] * 3,
        out_specs=(vmem, vmem),
        scratch_shapes=[
            pltpu.VMEM((2, users, rows, width), bf16),
            pltpu.VMEM((group, 1, rows), jnp.int32),
            pltpu.VMEM((length, rows, group * rows), f32),
            pltpu.VMEM((feats - 1, length, quarter, group * rows), f32),
            pltpu.VMEM((length, 8, length * quarter), f32),
            pltpu.VMEM((group, feats, 8, group * rows), f32),
            pltpu.VMEM((group, length, quarter, rows), bf16),
            pltpu.VMEM((length, group, rows, rows), bf16),
            pltpu.VMEM((users, rows, rows), bf16),
            dma((3,)),
            dma((2, users, 2)),
            dma((length, 2, 2)),
            dma((2, length - 1)),
            dma((2, length, group - 1)),
            dma((group - 1,)), dma((group - 1,)),
            dma((feats - 1, length)), dma((feats - 1, length)),
            dma((length - 1,)), dma((length - 1,)),
            dma((plane - 1,)), dma((plane - 1,)),
            dma((plane - 1,)), dma((plane - 1,)),
            dma((length - 1,)), dma((length - 1,)),
            dma((feats - 1,)), dma((feats - 1,)),
        ],
        compiler_params=pltpu.CompilerParams(
            collective_id=0, has_side_effects=True, vmem_limit_bytes=VMEM_BYTES),
        cost_estimate=pl.CostEstimate(
            flops=6 * users * rows * rows * width, bytes_accessed=16 * rows * width,
            transcendentals=4 * users * quarter * rows),
    )(view_one, view_two, partner.reshape(1, rows))
    return pl.pallas_call(
        hand_out,
        out_shape=(out, out),
        in_specs=[anywhere, anywhere],
        out_specs=(anywhere, anywhere),
        scratch_shapes=[pltpu.VMEM((2, rows, width), f32), dma((2, 2)), dma((2, 2))],
        compiler_params=pltpu.CompilerParams(vmem_limit_bytes=VMEM_BYTES),
    )(*grads)


def solution(mesh):
    return jax.shard_map(
        functools.partial(on_device, mesh.shape["user"], mesh.shape["feat"]),
        mesh=mesh,
        in_specs=(P("user", "feat"), P("user", "feat"), P("user")),
        out_specs=(P("user", "feat"), P("user", "feat")),
        check_vma=False,
    )
```

```python
import functools
import math

import jax
import jax.numpy as jnp
from jax import lax
from jax.experimental import pallas as pl
from jax.experimental.pallas import tpu as pltpu
from jax.sharding import PartitionSpec as P

D = 2048
VMEM_BYTES = 60 * 1024 * 1024
PIECES = (2, 1)
MESH = pl.DeviceIdType.MESH
NT = (((1,), (1,)), ((), ()))
TN = (((0,), (0,)), ((), ()))


def line_length(users):
    length = 1
    while length * length < users:
        length *= 2
    return length


def kernel(users, feats, one_ref, two_ref, partner_ref, g1_ref, g2_ref,
           views, partners, part, rs, colst, rowst, stage, coup, cols,
           local_sem, view_recv, line_send, group_send, partner_send, partner_recv,
           rs_send, rs_recv, col_send, col_recv, row_send, row_recv,
           coup_send, coup_recv, turn_send, turn_recv, cols_send, cols_recv):
    rows, width = one_ref.shape
    quarter = rows // feats
    length = line_length(users)
    group = users // length
    plane = group * feats
    scale = 2.0 / math.sqrt(D)
    u = lax.axis_index("user")
    f = lax.axis_index("feat")
    z = u // group
    y = lax.rem(u, group)
    mine = pl.ds(pl.multiple_of(f * quarter, quarter), quarter)

    loads = [pltpu.make_async_copy(ref, views.at[v, u], local_sem.at[v])
             for v, ref in enumerate((two_ref, one_ref))]
    loads.append(pltpu.make_async_copy(partner_ref, partners.at[y], local_sem.at[2]))
    for load in loads:
        load.start()

    def line_at(k):
        return lax.rem(z + k, length)

    def plane_at(p):
        return lax.rem(y + p // feats, group), lax.rem(f + p % feats, feats)

    barrier = pltpu.get_barrier_semaphore()
    for k in range(1, length):
        pl.semaphore_signal(barrier, inc=1, device_id=(line_at(k) * group + y, f), device_id_type=MESH)
    for p in range(1, plane):
        to_y, to_f = plane_at(p)
        pl.semaphore_signal(barrier, inc=1, device_id=(z * group + to_y, to_f), device_id_type=MESH)
    pl.semaphore_wait(barrier, length + plane - 2)

    def remote(src, dst, send, recv, to_z, to_y, to_f):
        return pltpu.make_async_remote_copy(
            src_ref=src, dst_ref=dst, send_sem=send, recv_sem=recv,
            device_id=(to_z * group + to_y, to_f), device_id_type=MESH)

    def piece(v, b, h):
        size = rows // PIECES[v]
        return views.at[v, b, pl.ds(h * size, size)]

    def along(v, src, step, h):
        b = src * group + y
        return remote(piece(v, b, h), piece(v, b, h), line_send.at[v, src, (step + 1) // 2, h],
                      view_recv.at[v, b, h], z + step, y, f)

    def across(v, src, k):
        b = src * group + y
        return remote(views.at[v, b], views.at[v, b], group_send.at[v, src, k - 1],
                      view_recv.at[v, b, 0], z, lax.rem(y + k, group), f)

    def arrived(v, b):
        remote(views.at[v, b], views.at[v, b], line_send.at[0, 0, 0, 0], view_recv.at[v, b, 0], z, y, f).wait_recv()

    def each_on_line(d, body):
        for step in ((1, -1) if d else (0,)):
            src = z + step * d

            @pl.when((src >= 0) & (src < length))
            def _():
                body(src, step)

    def onward(step, act):
        for way in ((-step,) if step else (1, -1)):
            @pl.when((z + way >= 0) & (z + way < length))
            def _():
                act(way)

    def pass_on(v, d):
        for h in range(PIECES[v]):
            def body(src, step):
                if d:
                    along(v, src, step, h).wait_recv()
                onward(step, lambda way: along(v, src, way, h).start())
            each_on_line(d, body)

    def cross(v, d):
        def body(src, step):
            for k in range(1, group):
                across(v, src, k).start()
        each_on_line(d, body)

    def sent(v):
        for d in range(length):
            def body(src, step):
                for h in range(PIECES[v]):
                    onward(step, lambda way: along(v, src, way, h).wait_send())
                for k in range(1, group):
                    across(v, src, k).wait_send()
            each_on_line(d, body)

    def crossed(v):
        def one(src, carry):
            for k in range(1, group):
                arrived(v, src * group + lax.rem(y + k, group))
            return carry
        lax.fori_loop(0, length, one, 0)

    def partner_copy(k):
        return remote(partners.at[y], partners.at[y], partner_send.at[k - 1], partner_recv.at[k - 1],
                      z, lax.rem(y + k, group), f)

    def rs_copy(src, k):
        to = lax.rem(f + k, feats)
        return remote(part.at[src, pl.ds(pl.multiple_of(to * quarter, quarter), quarter)], rs.at[k - 1, src],
                      rs_send.at[k - 1, src], rs_recv.at[k - 1, src], z, y, to)

    def score(d):
        def body(src, step):
            part[src] = lax.dot_general(
                views[0, src * group + y], views[1, pl.ds(z * group, group)].reshape(group * rows, width),
                NT, preferred_element_type=jnp.float32)
            for k in range(1, feats):
                rs_copy(src, k).start()
        each_on_line(d, body)

    loads[0].wait()
    pass_on(0, 0)
    loads[1].wait()
    cross(1, 0)
    loads[2].wait()
    for k in range(1, group):
        partner_copy(k).start()
    cross(0, 0)
    for k in range(1, group):
        arrived(1, z * group + lax.rem(y + k, group))
    score(0)
    for d in range(1, length):
        pass_on(0, d)
        if d == max(length - 2, 1):
            pass_on(1, 0)
        score(d)
        cross(0, d)
    pass_on(1, 1)
    cross(1, 1)

    def rs_wait(src, carry):
        for k in range(1, feats):
            rs_copy(src, k).wait_recv()
        return carry
    lax.fori_loop(0, length, rs_wait, 0)
    total = part[:, mine, :]
    for k in range(feats - 1):
        total = total + rs[k]
    scores = (scale * total).reshape(length * quarter, group * rows)
    scores_t = scores.T

    row_high = jnp.max(scores, axis=0, keepdims=True)
    row_exp = jnp.exp(scores - row_high)
    rowst[y, f, 0:1] = row_high
    rowst[y, f, 1:2] = jnp.sum(row_exp, axis=0, keepdims=True)
    col_high = jnp.max(scores_t, axis=0, keepdims=True)
    col_exp = jnp.exp(scores_t - col_high)
    colst[z, 0:1] = col_high
    colst[z, 1:2] = jnp.sum(col_exp, axis=0, keepdims=True)

    def col_copy(k):
        return remote(colst.at[z], colst.at[z], col_send.at[k - 1], col_recv.at[k - 1], line_at(k), y, f)

    def row_copy(p):
        return remote(rowst.at[y, f], rowst.at[y, f], row_send.at[p - 1], row_recv.at[p - 1], z, *plane_at(p))

    for k in range(1, length):
        col_copy(k).start()
    for p in range(1, plane):
        row_copy(p).start()
    pass_on(1, 2)
    cross(1, 2)
    for k in range(1, group):
        partner_copy(k).wait_recv()
    for p in range(1, plane):
        row_copy(p).wait_recv()
    for k in range(1, length):
        col_copy(k).wait_recv()

    def share(own, stats):
        high = functools.reduce(jnp.maximum, [highest for highest, _ in stats])
        whole = sum(value * jnp.exp(highest - high) for highest, value in stats)
        return 0.5 * jnp.exp(own - (high + jnp.log(whole)))

    row_share = share(row_high, [(rowst[i, j, 0:1], rowst[i, j, 1:2]) for i in range(group) for j in range(feats)])
    col_share = share(col_high, [(colst[i, 0:1], colst[i, 1:2]) for i in range(length)])
    both = row_exp * row_share + (col_exp * col_share).T
    block = (length, quarter, rows)
    index = (lax.broadcasted_iota(jnp.int32, block, 0) * (group * rows)
             + lax.broadcasted_iota(jnp.int32, block, 1) + (y * rows + f * quarter))
    for i in range(group):
        hit = jnp.where(index == partners[i].reshape(1, 1, rows), 1.0, 0.0)
        stage[i] = (both[:, i * rows:(i + 1) * rows].reshape(block) - hit).astype(jnp.bfloat16)

    def turn_copy(k):
        return remote(stage.at[:, line_at(k)], cols.at[pl.ds(z * group, group), mine],
                      turn_send.at[k - 1], turn_recv.at[k - 1], line_at(k), y, f)

    def coup_copy(p):
        to_y, to_f = plane_at(p)
        return remote(stage.at[to_y], coup.at[:, y, mine], coup_send.at[p - 1], coup_recv.at[p - 1], z, to_y, to_f)

    def cols_copy(k):
        return remote(cols.at[:, mine], cols.at[:, mine],
                      cols_send.at[k - 1], cols_recv.at[k - 1], z, y, lax.rem(f + k, feats))

    for k in range(1, length):
        turn_copy(k).start()
    for p in range(1, plane):
        coup_copy(p).start()
    coup[:, y, mine, :] = stage[y]
    cols[pl.ds(z * group, group), mine, :] = stage[:, z]
    for d in range(3, length):
        pass_on(1, d)
        cross(1, d)
    for k in range(1, length):
        turn_copy(k).wait_recv()
    for k in range(1, feats):
        cols_copy(k).start()

    def summed(out_ref, term):
        chunk = math.gcd(users, 8)
        out_ref[...] = term(0, chunk)

        def step(c, carry):
            out_ref[...] += term(c * chunk, chunk)
            return carry
        if users > chunk:
            lax.fori_loop(1, users // chunk, step, 0)

    def one_term(b, chunk):
        left = coup[pl.ds(b // group, chunk // group)].reshape(chunk * rows, rows)
        return lax.dot_general(left, views[0, pl.ds(b, chunk)].reshape(chunk * rows, width),
                               TN, preferred_element_type=jnp.float32)

    def two_term(b, chunk):
        left = jnp.concatenate([cols[b + i] for i in range(chunk)], axis=1)
        return jnp.dot(left, views[1, pl.ds(b, chunk)].reshape(chunk * rows, width),
                       preferred_element_type=jnp.float32)

    for p in range(1, plane):
        coup_copy(p).wait_recv()
    crossed(0)
    summed(g1_ref, one_term)

    def late(src, carry):
        @pl.when(src != z)
        def _():
            for k in range(1, group):
                arrived(1, src * group + lax.rem(y + k, group))
        return carry
    lax.fori_loop(0, length, late, 0)
    for k in range(1, feats):
        cols_copy(k).wait_recv()
    summed(g2_ref, two_term)

    sent(0)
    sent(1)

    def rs_sent(src, carry):
        for k in range(1, feats):
            rs_copy(src, k).wait_send()
        return carry
    lax.fori_loop(0, length, rs_sent, 0)
    for k in range(1, group):
        partner_copy(k).wait_send()
    for k in range(1, length):
        col_copy(k).wait_send()
        turn_copy(k).wait_send()
    for p in range(1, plane):
        row_copy(p).wait_send()
        coup_copy(p).wait_send()
    for k in range(1, feats):
        cols_copy(k).wait_send()


def hand_out(one_ref, two_ref, one_out, two_out, held, come, go):
    rows = held.shape[1] // 2
    parts = [(v, h, ref.at[pl.ds(h * rows, rows)], out.at[pl.ds(h * rows, rows)], held.at[v, pl.ds(h * rows, rows)])
             for v, (ref, out) in enumerate(((one_ref, one_out), (two_ref, two_out))) for h in range(2)]
    ins = [pltpu.make_async_copy(src, slot, come.at[v, h]) for v, h, src, _, slot in parts]
    outs = [pltpu.make_async_copy(slot, dst, go.at[v, h]) for v, h, _, dst, slot in parts]
    for copy in ins:
        copy.start()
    for copy, out in zip(ins, outs):
        copy.wait()
        out.start()
    for out in outs:
        out.wait()


def on_device(users, feats, view_one, view_two, partner):
    rows, width = view_one.shape
    quarter = rows // feats
    length = line_length(users)
    group = users // length
    plane = group * feats
    out = jax.ShapeDtypeStruct((rows, width), jnp.float32)
    vmem = pl.BlockSpec(memory_space=pltpu.VMEM)
    anywhere = pl.BlockSpec(memory_space=pl.ANY)
    dma = pltpu.SemaphoreType.DMA
    f32, bf16 = jnp.float32, jnp.bfloat16
    grads = pl.pallas_call(
        functools.partial(kernel, users, feats),
        out_shape=(out, out),
        in_specs=[anywhere] * 3,
        out_specs=(vmem, vmem),
        scratch_shapes=[
            pltpu.VMEM((2, users, rows, width), bf16),
            pltpu.VMEM((group, 1, rows), jnp.int32),
            pltpu.VMEM((length, rows, group * rows), f32),
            pltpu.VMEM((feats - 1, length, quarter, group * rows), f32),
            pltpu.VMEM((length, 8, length * quarter), f32),
            pltpu.VMEM((group, feats, 8, group * rows), f32),
            pltpu.VMEM((group, length, quarter, rows), bf16),
            pltpu.VMEM((length, group, rows, rows), bf16),
            pltpu.VMEM((users, rows, rows), bf16),
            dma((3,)),
            dma((2, users, 2)),
            dma((2, length, 2, 2)),
            dma((2, length, group - 1)),
            dma((group - 1,)), dma((group - 1,)),
            dma((feats - 1, length)), dma((feats - 1, length)),
            dma((length - 1,)), dma((length - 1,)),
            dma((plane - 1,)), dma((plane - 1,)),
            dma((plane - 1,)), dma((plane - 1,)),
            dma((length - 1,)), dma((length - 1,)),
            dma((feats - 1,)), dma((feats - 1,)),
        ],
        compiler_params=pltpu.CompilerParams(
            collective_id=0, has_side_effects=True, vmem_limit_bytes=VMEM_BYTES),
        cost_estimate=pl.CostEstimate(
            flops=6 * users * rows * rows * width, bytes_accessed=16 * rows * width,
            transcendentals=4 * users * quarter * rows),
    )(view_one, view_two, partner.reshape(1, rows))
    return pl.pallas_call(
        hand_out,
        out_shape=(out, out),
        in_specs=[anywhere, anywhere],
        out_specs=(anywhere, anywhere),
        scratch_shapes=[pltpu.VMEM((2, rows, width), f32), dma((2, 2)), dma((2, 2))],
        compiler_params=pltpu.CompilerParams(vmem_limit_bytes=VMEM_BYTES),
    )(*grads)


def solution(mesh):
    return jax.shard_map(
        functools.partial(on_device, mesh.shape["user"], mesh.shape["feat"]),
        mesh=mesh,
        in_specs=(P("user", "feat"), P("user", "feat"), P("user")),
        out_specs=(P("user", "feat"), P("user", "feat")),
        check_vma=False,
    )
```

```python
import functools
import math

import jax
import jax.numpy as jnp
from jax import lax
from jax.experimental import pallas as pl
from jax.experimental.pallas import tpu as pltpu
from jax.sharding import PartitionSpec as P

D = 2048
VMEM_BYTES = 60 * 1024 * 1024
PIECES = 2
MESH = pl.DeviceIdType.MESH
NT = (((1,), (1,)), ((), ()))
TN = (((0,), (0,)), ((), ()))


def line_length(users):
    length = 1
    while length * length < users:
        length *= 2
    return length


def kernel(users, feats, one_ref, two_ref, partner_ref, g1_out, g2_out,
           views, partners, part, rs, colst, rowst, stage, coup, cols, g1_ref, g2_ref,
           out_sem, local_sem, view_recv, line_send, group_send, partner_send, partner_recv,
           rs_send, rs_recv, col_send, col_recv, row_send, row_recv,
           coup_send, coup_recv, turn_send, turn_recv, cols_send, cols_recv):
    rows, width = one_ref.shape
    quarter = rows // feats
    length = line_length(users)
    group = users // length
    plane = group * feats
    scale = 2.0 / math.sqrt(D)
    u = lax.axis_index("user")
    f = lax.axis_index("feat")
    z = u // group
    y = lax.rem(u, group)
    mine = pl.ds(pl.multiple_of(f * quarter, quarter), quarter)

    loads = [pltpu.make_async_copy(ref, views.at[v, u], local_sem.at[v])
             for v, ref in enumerate((two_ref, one_ref))]
    loads.append(pltpu.make_async_copy(partner_ref, partners.at[y], local_sem.at[2]))
    for load in loads:
        load.start()

    def line_at(k):
        return lax.rem(z + k, length)

    def plane_at(p):
        return lax.rem(y + p // feats, group), lax.rem(f + p % feats, feats)

    barrier = pltpu.get_barrier_semaphore()
    for k in range(1, length):
        pl.semaphore_signal(barrier, inc=1, device_id=(line_at(k) * group + y, f), device_id_type=MESH)
    for p in range(1, plane):
        to_y, to_f = plane_at(p)
        pl.semaphore_signal(barrier, inc=1, device_id=(z * group + to_y, to_f), device_id_type=MESH)
    pl.semaphore_wait(barrier, length + plane - 2)

    def remote(src, dst, send, recv, to_z, to_y, to_f):
        return pltpu.make_async_remote_copy(
            src_ref=src, dst_ref=dst, send_sem=send, recv_sem=recv,
            device_id=(to_z * group + to_y, to_f), device_id_type=MESH)

    def piece(v, b, h):
        size = rows // PIECES
        return views.at[v, b, pl.ds(h * size, size)]

    def along(v, src, step, h):
        b = src * group + y
        return remote(piece(v, b, h), piece(v, b, h), line_send.at[v, src, (step + 1) // 2, h],
                      view_recv.at[v, b, h], z + step, y, f)

    def across(v, src, k, h):
        b = src * group + y
        return remote(piece(v, b, h), piece(v, b, h), group_send.at[v, src, k - 1, h],
                      view_recv.at[v, b, h], z, lax.rem(y + k, group), f)

    def arrived(v, b):
        for h in range(PIECES):
            remote(piece(v, b, h), piece(v, b, h), line_send.at[0, 0, 0, 0], view_recv.at[v, b, h], z, y, f).wait_recv()

    def each_on_line(d, body):
        for step in ((1, -1) if d else (0,)):
            src = z + step * d

            @pl.when((src >= 0) & (src < length))
            def _():
                body(src, step)

    def onward(step, act):
        for way in ((-step,) if step else (1, -1)):
            @pl.when((z + way >= 0) & (z + way < length))
            def _():
                act(way)

    def pass_on(v, d):
        for h in range(PIECES):
            def body(src, step):
                if d:
                    along(v, src, step, h).wait_recv()
                onward(step, lambda way: along(v, src, way, h).start())
                if v and d:
                    for k in range(1, group):
                        across(v, src, k, h).start()
            each_on_line(d, body)

    def cross(v, d):
        def body(src, step):
            for h in range(PIECES):
                for k in range(1, group):
                    across(v, src, k, h).start()
        each_on_line(d, body)

    def sent(v):
        for d in range(length):
            def body(src, step):
                for h in range(PIECES):
                    onward(step, lambda way: along(v, src, way, h).wait_send())
                    for k in range(1, group):
                        across(v, src, k, h).wait_send()
            each_on_line(d, body)

    def crossed(v):
        def one(src, carry):
            for k in range(1, group):
                arrived(v, src * group + lax.rem(y + k, group))
            return carry
        lax.fori_loop(0, length, one, 0)

    def partner_copy(k):
        return remote(partners.at[y], partners.at[y], partner_send.at[k - 1], partner_recv.at[k - 1],
                      z, lax.rem(y + k, group), f)

    def rs_copy(src, k):
        to = lax.rem(f + k, feats)
        return remote(part.at[src, pl.ds(pl.multiple_of(to * quarter, quarter), quarter)], rs.at[k - 1, src],
                      rs_send.at[k - 1, src], rs_recv.at[k - 1, src], z, y, to)

    def score(d):
        def body(src, step):
            part[src] = lax.dot_general(
                views[0, src * group + y], views[1, pl.ds(z * group, group)].reshape(group * rows, width),
                NT, preferred_element_type=jnp.float32)
            for k in range(1, feats):
                rs_copy(src, k).start()
        each_on_line(d, body)

    loads[0].wait()
    pass_on(0, 0)
    loads[1].wait()
    cross(1, 0)
    loads[2].wait()
    for k in range(1, group):
        partner_copy(k).start()
    cross(0, 0)
    for k in range(1, group):
        arrived(1, z * group + lax.rem(y + k, group))
    score(0)
    for d in range(1, length):
        pass_on(0, d)
        if d == max(length - 2, 1):
            pass_on(1, 0)
        score(d)
        cross(0, d)
    pass_on(1, 1)

    def rs_wait(src, carry):
        for k in range(1, feats):
            rs_copy(src, k).wait_recv()
        return carry
    lax.fori_loop(0, length, rs_wait, 0)
    total = part[:, mine, :]
    for k in range(feats - 1):
        total = total + rs[k]
    scores = (scale * total).reshape(length * quarter, group * rows)
    scores_t = scores.T

    row_high = jnp.max(scores, axis=0, keepdims=True)
    row_exp = jnp.exp(scores - row_high)
    rowst[y, f, 0:1] = row_high
    rowst[y, f, 1:2] = jnp.sum(row_exp, axis=0, keepdims=True)
    col_high = jnp.max(scores_t, axis=0, keepdims=True)
    col_exp = jnp.exp(scores_t - col_high)
    colst[z, 0:1] = col_high
    colst[z, 1:2] = jnp.sum(col_exp, axis=0, keepdims=True)

    def col_copy(k):
        return remote(colst.at[z], colst.at[z], col_send.at[k - 1], col_recv.at[k - 1], line_at(k), y, f)

    def row_copy(p):
        return remote(rowst.at[y, f], rowst.at[y, f], row_send.at[p - 1], row_recv.at[p - 1], z, *plane_at(p))

    for k in range(1, length):
        col_copy(k).start()
    for p in range(1, plane):
        row_copy(p).start()
    pass_on(1, 2)
    for k in range(1, group):
        partner_copy(k).wait_recv()
    for p in range(1, plane):
        row_copy(p).wait_recv()
    for k in range(1, length):
        col_copy(k).wait_recv()

    def share(own, stats):
        high = functools.reduce(jnp.maximum, [highest for highest, _ in stats])
        whole = sum(value * jnp.exp(highest - high) for highest, value in stats)
        return 0.5 * jnp.exp(own - (high + jnp.log(whole)))

    row_share = share(row_high, [(rowst[i, j, 0:1], rowst[i, j, 1:2]) for i in range(group) for j in range(feats)])
    col_share = share(col_high, [(colst[i, 0:1], colst[i, 1:2]) for i in range(length)])
    both = row_exp * row_share + (col_exp * col_share).T
    block = (length, quarter, rows)
    index = (lax.broadcasted_iota(jnp.int32, block, 0) * (group * rows)
             + lax.broadcasted_iota(jnp.int32, block, 1) + (y * rows + f * quarter))
    for i in range(group):
        hit = jnp.where(index == partners[i].reshape(1, 1, rows), 1.0, 0.0)
        stage[i] = (both[:, i * rows:(i + 1) * rows].reshape(block) - hit).astype(jnp.bfloat16)

    def turn_copy(k):
        return remote(stage.at[:, line_at(k)], cols.at[pl.ds(z * group, group), mine],
                      turn_send.at[k - 1], turn_recv.at[k - 1], line_at(k), y, f)

    def coup_copy(p):
        to_y, to_f = plane_at(p)
        return remote(stage.at[to_y], coup.at[:, y, mine], coup_send.at[p - 1], coup_recv.at[p - 1], z, to_y, to_f)

    def cols_copy(k):
        return remote(cols.at[:, mine], cols.at[:, mine],
                      cols_send.at[k - 1], cols_recv.at[k - 1], z, y, lax.rem(f + k, feats))

    for k in range(1, length):
        turn_copy(k).start()
    for p in range(1, plane):
        coup_copy(p).start()
    coup[:, y, mine, :] = stage[y]
    cols[pl.ds(z * group, group), mine, :] = stage[:, z]
    for d in range(3, length):
        pass_on(1, d)
    for k in range(1, length):
        turn_copy(k).wait_recv()
    for k in range(1, feats):
        cols_copy(k).start()

    def summed(out_ref, term):
        chunk = math.gcd(users, 8)
        out_ref[...] = term(0, chunk)

        def step(c, carry):
            out_ref[...] += term(c * chunk, chunk)
            return carry
        if users > chunk:
            lax.fori_loop(1, users // chunk, step, 0)

    def one_term(b, chunk):
        left = coup[pl.ds(b // group, chunk // group)].reshape(chunk * rows, rows)
        return lax.dot_general(left, views[0, pl.ds(b, chunk)].reshape(chunk * rows, width),
                               TN, preferred_element_type=jnp.float32)

    def two_term(b, chunk):
        left = jnp.concatenate([cols[b + i] for i in range(chunk)], axis=1)
        return jnp.dot(left, views[1, pl.ds(b, chunk)].reshape(chunk * rows, width),
                       preferred_element_type=jnp.float32)

    for p in range(1, plane):
        coup_copy(p).wait_recv()
    crossed(0)
    summed(g1_ref, one_term)
    leave_one = pltpu.make_async_copy(g1_ref, g1_out, out_sem.at[0])
    leave_one.start()

    def late(src, carry):
        @pl.when(src != z)
        def _():
            for k in range(1, group):
                arrived(1, src * group + lax.rem(y + k, group))
        return carry
    lax.fori_loop(0, length, late, 0)
    for k in range(1, feats):
        cols_copy(k).wait_recv()
    summed(g2_ref, two_term)
    leave_two = pltpu.make_async_copy(g2_ref, g2_out, out_sem.at[1])
    leave_two.start()

    sent(0)
    sent(1)

    def rs_sent(src, carry):
        for k in range(1, feats):
            rs_copy(src, k).wait_send()
        return carry
    lax.fori_loop(0, length, rs_sent, 0)
    for k in range(1, group):
        partner_copy(k).wait_send()
    for k in range(1, length):
        col_copy(k).wait_send()
        turn_copy(k).wait_send()
    for p in range(1, plane):
        row_copy(p).wait_send()
        coup_copy(p).wait_send()
    for k in range(1, feats):
        cols_copy(k).wait_send()
    leave_one.wait()
    leave_two.wait()


def hand_out(one_ref, two_ref, one_out, two_out, held, come, go):
    rows = held.shape[1] // 2
    parts = [(v, h, ref.at[pl.ds(h * rows, rows)], out.at[pl.ds(h * rows, rows)], held.at[v, pl.ds(h * rows, rows)])
             for v, (ref, out) in enumerate(((one_ref, one_out), (two_ref, two_out))) for h in range(2)]
    ins = [pltpu.make_async_copy(src, slot, come.at[v, h]) for v, h, src, _, slot in parts]
    outs = [pltpu.make_async_copy(slot, dst, go.at[v, h]) for v, h, _, dst, slot in parts]
    for copy in ins:
        copy.start()
    for copy, out in zip(ins, outs):
        copy.wait()
        out.start()
    for out in outs:
        out.wait()


def on_device(users, feats, view_one, view_two, partner):
    rows, width = view_one.shape
    quarter = rows // feats
    length = line_length(users)
    group = users // length
    plane = group * feats
    out = jax.ShapeDtypeStruct((rows, width), jnp.float32)
    anywhere = pl.BlockSpec(memory_space=pl.ANY)
    dma = pltpu.SemaphoreType.DMA
    f32, bf16 = jnp.float32, jnp.bfloat16
    grads = pl.pallas_call(
        functools.partial(kernel, users, feats),
        out_shape=(out, out),
        in_specs=[anywhere] * 3,
        out_specs=(anywhere, anywhere),
        scratch_shapes=[
            pltpu.VMEM((2, users, rows, width), bf16),
            pltpu.VMEM((group, 1, rows), jnp.int32),
            pltpu.VMEM((length, rows, group * rows), f32),
            pltpu.VMEM((feats - 1, length, quarter, group * rows), f32),
            pltpu.VMEM((length, 8, length * quarter), f32),
            pltpu.VMEM((group, feats, 8, group * rows), f32),
            pltpu.VMEM((group, length, quarter, rows), bf16),
            pltpu.VMEM((length, group, rows, rows), bf16),
            pltpu.VMEM((users, rows, rows), bf16),
            pltpu.VMEM((rows, width), f32),
            pltpu.VMEM((rows, width), f32),
            dma((2,)),
            dma((3,)),
            dma((2, users, PIECES)),
            dma((2, length, 2, PIECES)),
            dma((2, length, group - 1, PIECES)),
            dma((group - 1,)), dma((group - 1,)),
            dma((feats - 1, length)), dma((feats - 1, length)),
            dma((length - 1,)), dma((length - 1,)),
            dma((plane - 1,)), dma((plane - 1,)),
            dma((plane - 1,)), dma((plane - 1,)),
            dma((length - 1,)), dma((length - 1,)),
            dma((feats - 1,)), dma((feats - 1,)),
        ],
        compiler_params=pltpu.CompilerParams(
            collective_id=0, has_side_effects=True, vmem_limit_bytes=VMEM_BYTES),
        cost_estimate=pl.CostEstimate(
            flops=6 * users * rows * rows * width, bytes_accessed=16 * rows * width,
            transcendentals=4 * users * quarter * rows),
    )(view_one, view_two, partner.reshape(1, rows))
    return pl.pallas_call(
        hand_out,
        out_shape=(out, out),
        in_specs=[anywhere, anywhere],
        out_specs=(anywhere, anywhere),
        scratch_shapes=[pltpu.VMEM((2, rows, width), f32), dma((2, 2)), dma((2, 2))],
        compiler_params=pltpu.CompilerParams(vmem_limit_bytes=VMEM_BYTES),
    )(*grads)


def solution(mesh):
    return jax.shard_map(
        functools.partial(on_device, mesh.shape["user"], mesh.shape["feat"]),
        mesh=mesh,
        in_specs=(P("user", "feat"), P("user", "feat"), P("user")),
        out_specs=(P("user", "feat"), P("user", "feat")),
        check_vma=False,
    )
```

```python
import functools
import math

import jax
import jax.numpy as jnp
from jax import lax
from jax.experimental import pallas as pl
from jax.experimental.pallas import tpu as pltpu
from jax.sharding import PartitionSpec as P

D = 2048
VMEM_BYTES = 60 * 1024 * 1024
PIECES = 2
MESH = pl.DeviceIdType.MESH
NT = (((1,), (1,)), ((), ()))
TN = (((0,), (0,)), ((), ()))


def line_length(users):
    length = 1
    while length * length < users:
        length *= 2
    return length


def kernel(users, feats, one_ref, two_ref, partner_ref, g1_out, g2_out,
           views, partners, part, rs, colst, rowst, stage, coup, cols, g1_ref, g2_ref,
           out_sem, local_sem, view_recv, line_send, group_send, partner_send, partner_recv,
           rs_send, rs_recv, col_send, col_recv, row_send, row_recv,
           coup_send, coup_recv, turn_send, turn_recv, cols_send, cols_recv):
    rows, width = one_ref.shape
    quarter = rows // feats
    length = line_length(users)
    group = users // length
    plane = group * feats
    scale = 2.0 / math.sqrt(D)
    u = lax.axis_index("user")
    f = lax.axis_index("feat")
    z = u // group
    y = lax.rem(u, group)
    mine = pl.ds(pl.multiple_of(f * quarter, quarter), quarter)

    loads = [pltpu.make_async_copy(ref, views.at[v, u], local_sem.at[v])
             for v, ref in enumerate((two_ref, one_ref))]
    loads.append(pltpu.make_async_copy(partner_ref, partners.at[y], local_sem.at[2]))
    for load in loads:
        load.start()

    def line_at(k):
        return lax.rem(z + k, length)

    def plane_at(p):
        return lax.rem(y + p // feats, group), lax.rem(f + p % feats, feats)

    barrier = pltpu.get_barrier_semaphore()
    for k in range(1, length):
        pl.semaphore_signal(barrier, inc=1, device_id=(line_at(k) * group + y, f), device_id_type=MESH)
    for p in range(1, plane):
        to_y, to_f = plane_at(p)
        pl.semaphore_signal(barrier, inc=1, device_id=(z * group + to_y, to_f), device_id_type=MESH)
    pl.semaphore_wait(barrier, length + plane - 2)

    def remote(src, dst, send, recv, to_z, to_y, to_f):
        return pltpu.make_async_remote_copy(
            src_ref=src, dst_ref=dst, send_sem=send, recv_sem=recv,
            device_id=(to_z * group + to_y, to_f), device_id_type=MESH)

    def piece(v, b, h):
        size = rows // PIECES
        return views.at[v, b, pl.ds(h * size, size)]

    def along(v, src, step, h):
        b = src * group + y
        return remote(piece(v, b, h), piece(v, b, h), line_send.at[v, src, (step + 1) // 2, h],
                      view_recv.at[v, b, h], z + step, y, f)

    def across(v, src, k, h):
        b = src * group + y
        return remote(piece(v, b, h), piece(v, b, h), group_send.at[v, src, k - 1, h],
                      view_recv.at[v, b, h], z, lax.rem(y + k, group), f)

    def arrived(v, b):
        for h in range(PIECES):
            remote(piece(v, b, h), piece(v, b, h), line_send.at[0, 0, 0, 0], view_recv.at[v, b, h], z, y, f).wait_recv()

    def each_on_line(d, body):
        for step in ((1, -1) if d else (0,)):
            src = z + step * d

            @pl.when((src >= 0) & (src < length))
            def _():
                body(src, step)

    def onward(step, act):
        for way in ((-step,) if step else (1, -1)):
            @pl.when((z + way >= 0) & (z + way < length))
            def _():
                act(way)

    def pass_on(v, d):
        for h in range(PIECES):
            def body(src, step):
                if d:
                    along(v, src, step, h).wait_recv()
                onward(step, lambda way: along(v, src, way, h).start())
                if v and d:
                    for k in range(1, group):
                        across(v, src, k, h).start()
            each_on_line(d, body)

    def cross(v, d):
        def body(src, step):
            for h in range(PIECES):
                for k in range(1, group):
                    across(v, src, k, h).start()
        each_on_line(d, body)

    def sent(v):
        for d in range(length):
            def body(src, step):
                for h in range(PIECES):
                    onward(step, lambda way: along(v, src, way, h).wait_send())
                    for k in range(1, group):
                        across(v, src, k, h).wait_send()
            each_on_line(d, body)

    def crossed(v):
        def one(src, carry):
            for k in range(1, group):
                arrived(v, src * group + lax.rem(y + k, group))
            return carry
        lax.fori_loop(0, length, one, 0)

    def partner_copy(k):
        return remote(partners.at[y], partners.at[y], partner_send.at[k - 1], partner_recv.at[k - 1],
                      z, lax.rem(y + k, group), f)

    def rs_copy(src, k):
        to = lax.rem(f + k, feats)
        return remote(part.at[src, pl.ds(pl.multiple_of(to * quarter, quarter), quarter)], rs.at[k - 1, src],
                      rs_send.at[k - 1, src], rs_recv.at[k - 1, src], z, y, to)

    def score(d):
        def body(src, step):
            part[src] = lax.dot_general(
                views[0, src * group + y], views[1, pl.ds(z * group, group)].reshape(group * rows, width),
                NT, preferred_element_type=jnp.float32)
            for k in range(1, feats):
                rs_copy(src, k).start()
        each_on_line(d, body)

    loads[0].wait()
    pass_on(0, 0)
    loads[1].wait()
    cross(1, 0)
    loads[2].wait()
    for k in range(1, group):
        partner_copy(k).start()
    cross(0, 0)
    for k in range(1, group):
        arrived(1, z * group + lax.rem(y + k, group))
    score(0)
    for d in range(1, length):
        pass_on(0, d)
        if d == max(length - 2, 1):
            pass_on(1, 0)
        score(d)
        cross(0, d)
    pass_on(1, 1)

    def rs_wait(src, carry):
        for k in range(1, feats):
            rs_copy(src, k).wait_recv()
        return carry
    lax.fori_loop(0, length, rs_wait, 0)
    total = part[:, mine, :]
    for k in range(feats - 1):
        total = total + rs[k]
    scores = (scale * total).reshape(length * quarter, group * rows)
    scores_t = scores.T

    row_high = jnp.max(scores, axis=0, keepdims=True)
    row_exp = jnp.exp(scores - row_high)
    rowst[y, f, 0:1] = row_high
    rowst[y, f, 1:2] = jnp.sum(row_exp, axis=0, keepdims=True)
    col_high = jnp.max(scores_t, axis=0, keepdims=True)
    col_exp = jnp.exp(scores_t - col_high)
    colst[z, 0:1] = col_high
    colst[z, 1:2] = jnp.sum(col_exp, axis=0, keepdims=True)

    def col_copy(k):
        return remote(colst.at[z], colst.at[z], col_send.at[k - 1], col_recv.at[k - 1], line_at(k), y, f)

    def row_copy(p):
        return remote(rowst.at[y, f], rowst.at[y, f], row_send.at[p - 1], row_recv.at[p - 1], z, *plane_at(p))

    for k in range(1, length):
        col_copy(k).start()
    for p in range(1, plane):
        row_copy(p).start()
    pass_on(1, 2)
    for k in range(1, group):
        partner_copy(k).wait_recv()
    for p in range(1, plane):
        row_copy(p).wait_recv()
    for k in range(1, length):
        col_copy(k).wait_recv()

    def share(own, stats):
        high = functools.reduce(jnp.maximum, [highest for highest, _ in stats])
        whole = sum(value * jnp.exp(highest - high) for highest, value in stats)
        return 0.5 * jnp.exp(own - (high + jnp.log(whole)))

    row_share = share(row_high, [(rowst[i, j, 0:1], rowst[i, j, 1:2]) for i in range(group) for j in range(feats)])
    col_share = share(col_high, [(colst[i, 0:1], colst[i, 1:2]) for i in range(length)])
    both = row_exp * row_share + (col_exp * col_share).T
    block = (length, quarter, rows)
    index = (lax.broadcasted_iota(jnp.int32, block, 0) * (group * rows)
             + lax.broadcasted_iota(jnp.int32, block, 1) + (y * rows + f * quarter))
    for i in range(group):
        hit = jnp.where(index == partners[i].reshape(1, 1, rows), 1.0, 0.0)
        stage[i] = (both[:, i * rows:(i + 1) * rows].reshape(block) - hit).astype(jnp.bfloat16)

    def turn_copy(k):
        return remote(stage.at[:, line_at(k)], cols.at[pl.ds(z * group, group), mine],
                      turn_send.at[k - 1], turn_recv.at[k - 1], line_at(k), y, f)

    def coup_copy(p):
        to_y, to_f = plane_at(p)
        return remote(stage.at[to_y], coup.at[:, y, mine], coup_send.at[p - 1], coup_recv.at[p - 1], z, to_y, to_f)

    def cols_copy(k):
        return remote(cols.at[:, mine], cols.at[:, mine],
                      cols_send.at[k - 1], cols_recv.at[k - 1], z, y, lax.rem(f + k, feats))

    for k in range(1, length):
        turn_copy(k).start()
    for p in range(1, plane):
        coup_copy(p).start()
    coup[:, y, mine, :] = stage[y]
    cols[pl.ds(z * group, group), mine, :] = stage[:, z]
    for k in range(1, length):
        turn_copy(k).wait_recv()
    for k in range(1, feats):
        cols_copy(k).start()
    for d in range(3, length):
        pass_on(1, d)

    def summed(out_ref, term):
        chunk = math.gcd(users, 8)
        out_ref[...] = term(0, chunk)

        def step(c, carry):
            out_ref[...] += term(c * chunk, chunk)
            return carry
        if users > chunk:
            lax.fori_loop(1, users // chunk, step, 0)

    def one_term(b, chunk):
        left = coup[pl.ds(b // group, chunk // group)].reshape(chunk * rows, rows)
        return lax.dot_general(left, views[0, pl.ds(b, chunk)].reshape(chunk * rows, width),
                               TN, preferred_element_type=jnp.float32)

    def two_term(b, chunk):
        left = jnp.concatenate([cols[b + i] for i in range(chunk)], axis=1)
        return jnp.dot(left, views[1, pl.ds(b, chunk)].reshape(chunk * rows, width),
                       preferred_element_type=jnp.float32)

    for p in range(1, plane):
        coup_copy(p).wait_recv()
    crossed(0)
    summed(g1_ref, one_term)
    leave_one = pltpu.make_async_copy(g1_ref, g1_out, out_sem.at[0])
    leave_one.start()

    def late(src, carry):
        @pl.when(src != z)
        def _():
            for k in range(1, group):
                arrived(1, src * group + lax.rem(y + k, group))
        return carry
    lax.fori_loop(0, length, late, 0)
    for k in range(1, feats):
        cols_copy(k).wait_recv()
    summed(g2_ref, two_term)
    leave_two = pltpu.make_async_copy(g2_ref, g2_out, out_sem.at[1])
    leave_two.start()

    sent(0)
    sent(1)

    def rs_sent(src, carry):
        for k in range(1, feats):
            rs_copy(src, k).wait_send()
        return carry
    lax.fori_loop(0, length, rs_sent, 0)
    for k in range(1, group):
        partner_copy(k).wait_send()
    for k in range(1, length):
        col_copy(k).wait_send()
        turn_copy(k).wait_send()
    for p in range(1, plane):
        row_copy(p).wait_send()
        coup_copy(p).wait_send()
    for k in range(1, feats):
        cols_copy(k).wait_send()
    leave_one.wait()
    leave_two.wait()


def hand_out(one_ref, two_ref, one_out, two_out, held, come, go):
    rows = held.shape[1] // 2
    parts = [(v, h, ref.at[pl.ds(h * rows, rows)], out.at[pl.ds(h * rows, rows)], held.at[v, pl.ds(h * rows, rows)])
             for v, (ref, out) in enumerate(((one_ref, one_out), (two_ref, two_out))) for h in range(2)]
    ins = [pltpu.make_async_copy(src, slot, come.at[v, h]) for v, h, src, _, slot in parts]
    outs = [pltpu.make_async_copy(slot, dst, go.at[v, h]) for v, h, _, dst, slot in parts]
    for copy in ins:
        copy.start()
    for copy, out in zip(ins, outs):
        copy.wait()
        out.start()
    for out in outs:
        out.wait()


def on_device(users, feats, view_one, view_two, partner):
    rows, width = view_one.shape
    quarter = rows // feats
    length = line_length(users)
    group = users // length
    plane = group * feats
    out = jax.ShapeDtypeStruct((rows, width), jnp.float32)
    anywhere = pl.BlockSpec(memory_space=pl.ANY)
    dma = pltpu.SemaphoreType.DMA
    f32, bf16 = jnp.float32, jnp.bfloat16
    grads = pl.pallas_call(
        functools.partial(kernel, users, feats),
        out_shape=(out, out),
        in_specs=[anywhere] * 3,
        out_specs=(anywhere, anywhere),
        scratch_shapes=[
            pltpu.VMEM((2, users, rows, width), bf16),
            pltpu.VMEM((group, 1, rows), jnp.int32),
            pltpu.VMEM((length, rows, group * rows), f32),
            pltpu.VMEM((feats - 1, length, quarter, group * rows), f32),
            pltpu.VMEM((length, 8, length * quarter), f32),
            pltpu.VMEM((group, feats, 8, group * rows), f32),
            pltpu.VMEM((group, length, quarter, rows), bf16),
            pltpu.VMEM((length, group, rows, rows), bf16),
            pltpu.VMEM((users, rows, rows), bf16),
            pltpu.VMEM((rows, width), f32),
            pltpu.VMEM((rows, width), f32),
            dma((2,)),
            dma((3,)),
            dma((2, users, PIECES)),
            dma((2, length, 2, PIECES)),
            dma((2, length, group - 1, PIECES)),
            dma((group - 1,)), dma((group - 1,)),
            dma((feats - 1, length)), dma((feats - 1, length)),
            dma((length - 1,)), dma((length - 1,)),
            dma((plane - 1,)), dma((plane - 1,)),
            dma((plane - 1,)), dma((plane - 1,)),
            dma((length - 1,)), dma((length - 1,)),
            dma((feats - 1,)), dma((feats - 1,)),
        ],
        compiler_params=pltpu.CompilerParams(
            collective_id=0, has_side_effects=True, vmem_limit_bytes=VMEM_BYTES),
        cost_estimate=pl.CostEstimate(
            flops=6 * users * rows * rows * width, bytes_accessed=16 * rows * width,
            transcendentals=4 * users * quarter * rows),
    )(view_one, view_two, partner.reshape(1, rows))
    return pl.pallas_call(
        hand_out,
        out_shape=(out, out),
        in_specs=[anywhere, anywhere],
        out_specs=(anywhere, anywhere),
        scratch_shapes=[pltpu.VMEM((2, rows, width), f32), dma((2, 2)), dma((2, 2))],
        compiler_params=pltpu.CompilerParams(vmem_limit_bytes=VMEM_BYTES),
    )(*grads)


def solution(mesh):
    return jax.shard_map(
        functools.partial(on_device, mesh.shape["user"], mesh.shape["feat"]),
        mesh=mesh,
        in_specs=(P("user", "feat"), P("user", "feat"), P("user")),
        out_specs=(P("user", "feat"), P("user", "feat")),
        check_vma=False,
    )
```
